32 devices in a mesh: arm: 4 (over x, core), space: 8 (over z, y).
Axes of the slice: x: 2, y: 2, z: 4, core: 2. Of those that a mesh axis runs over, the one named last changes fastest.
Arguments:
- fields: float32 [2, 32, 64, 128], P(None, 'space'), may hold values from -2.5 to 2.5
- starts: float32 [16, 32, 64, 128], P('arm', 'space'), may hold values from 0.6 to 1.4
- labels: int32 [16], P('arm'), may hold values from 0 to 1
Outputs:
- density: float32 [2, 32, 64, 128], P(None, 'space', 'arm')
- new_fields: float32 [2, 32, 64, 128], P(None, 'space', 'arm')
The draws below stay inside these ranges and needn't reach their ends.
All inputs are finite; a program needn't handle non-finite values.
Results may differ from the reference program's by a relative error of at most 0.0003.
Values sent between devices are 32-bit elements; how exact they have to be, the bound alone decides.
No kernel may reach another device: no remote copies, remote signals or barrier semaphores. Data moves between devices by JAX's collectives and lax.ppermute only.
A program may use at most 64 MiB of HBM per device.

```python
import jax
import jax.numpy as jnp
from jax import lax

NY = 64
NZ = 128
ARMS = 16
NX = 32


def draw_fields(key, part):
    key_rough, key_level = jax.random.split(key, 2)
    levels = jax.random.uniform(key_level, (2, NX, 1, 1), jnp.float32, -1.2, 1.2)
    roughness = 0.55 * jnp.clip(jax.random.normal(key_rough, (2, NX, NY, NZ), jnp.float32), -2.0, 2.0)
    return levels + roughness


def set_ends(result, own_key, smallest, largest):
    shape = result.shape
    spot = [jax.random.randint(jax.random.fold_in(own_key, axis), (), 0, shape[axis]) for axis in range(len(shape))]
    result = result.at[tuple(spot)].set(smallest)
    longest = shape.index(max(shape))
    spot[longest] = (spot[longest] + 1) % shape[longest]
    return result.at[tuple(spot)].set(largest)


def level_of(rng, shape, cuts, least, largest):
    def one(axis_at, shards_of):
        steps = jax.random.uniform(jax.random.fold_in(jax.random.fold_in(rng, 6), axis_at), (shards_of,), jnp.float32, least / len(cuts), largest / len(cuts))
        return jnp.repeat(jnp.exp(steps), shape[axis_at] // shards_of).reshape((-1,) + (1,) * (len(shape) - axis_at - 1))

    factor_of = one(*cuts[0])
    for cut in cuts[1:]:
        factor_of = factor_of * one(*cut)
    return factor_of


def setup_inputs(seed: int = 0) -> dict:
    streams_of = jax.random.split(jax.random.key(seed), 4)
    return {
        "fields": draw_fields(jax.random.fold_in(streams_of[3], 71), 0),
        "starts": jnp.clip(0.6 + 0.79999995 * jax.random.uniform(streams_of[1], (ARMS, NX, NY, NZ), jnp.float32) ** level_of(streams_of[1], (ARMS, NX, NY, NZ), ((0, 4), (1, 8)), -0.2, 0.2), 0.6, 1.4),
        "labels": set_ends(jax.random.randint(streams_of[2], (ARMS,), 0, 2), jax.random.fold_in(streams_of[2], 1), 0, 1).astype(jnp.int32),
    }


coupling_full = 0.15
contour_step = 0.05
chi_value = 2.0
mixing = 0.5


def stencil(values, coupling):
    beside = jnp.roll(values, 1, 0) + jnp.roll(values, -1, 0)
    beside = beside + jnp.roll(values, 1, 1) + jnp.roll(values, -1, 1)
    beside = beside + jnp.roll(values, 1, 2) + jnp.roll(values, -1, 2)
    return (1.0 - 6.0 * coupling) * values + coupling * beside


def substep(values, factor, coupling):
    return factor * stencil(factor * values, coupling)


def extrapolate(values, half_factor, full_factor):
    halves = substep(substep(values, half_factor, coupling_full / 2), half_factor, coupling_full / 2)
    whole_step = substep(values, full_factor, coupling_full)
    return (4.0 * halves - whole_step) / 3.0


def factors(fields, arm_label):
    field_arm = jnp.where(arm_label == 0, fields[0], fields[1])
    return jnp.exp(-field_arm * (contour_step / 4)), jnp.exp(-field_arm * (contour_step / 2))


def reference(fields, starts, labels):
    def forward(inputs):
        arm_label, initial = inputs
        half_factor, full_factor = factors(fields, arm_label)
        step_one = extrapolate(initial, half_factor, full_factor)
        step_two = extrapolate(step_one, half_factor, full_factor)
        return step_one, step_two

    step_ones, step_twos = lax.map(forward, (labels, starts))
    junction = jnp.prod(step_twos, axis=0)
    partition = jnp.mean(junction)

    def backward(inputs):
        arm_label, step_one, step_two = inputs
        half_factor, full_factor = factors(fields, arm_label)
        back_one = extrapolate(junction / step_two, half_factor, full_factor)
        back_two = extrapolate(back_one, half_factor, full_factor)
        segment = 0.25 * back_two + 0.5 * step_one * back_one + 0.25 * junction
        return segment / (ARMS * partition)

    segments = lax.map(backward, (labels, step_ones, step_twos))
    is_type_a = (labels == 0)[:, None, None, None]
    dens_a = jnp.sum(jnp.where(is_type_a, segments, 0.0), axis=0)
    dens_b = jnp.sum(jnp.where(is_type_a, 0.0, segments), axis=0)
    density = jnp.stack([dens_a, dens_b])
    pressure = 0.5 * (fields[0] + fields[1] - chi_value)
    update_a = fields[0] + mixing * (chi_value * dens_b + pressure - fields[0])
    update_b = fields[1] + mixing * (chi_value * dens_a + pressure - fields[1])
    return density, jnp.stack([update_a, update_b])
```

```python
import functools

import jax
import jax.numpy as jnp
from jax import lax
from jax.experimental import pallas as pl
from jax.experimental.pallas import tpu as pltpu
from jax.sharding import PartitionSpec as P

coupling_full = 0.15
contour_step = 0.05
chi_value = 2.0
mixing = 0.5
reach = 2

AXES = ("arm", "space")


def beside(plane):
    rows, columns = plane.shape
    total = pltpu.roll(plane, 1, 0) + pltpu.roll(plane, rows - 1, 0)
    return total + (pltpu.roll(plane, 1, 1) + pltpu.roll(plane, columns - 1, 1))


def contour(first, last, arms, factor, values, store, p_ref, t_ref, s_ref):
    half = coupling_full / 2
    centre_half, centre_full = 1.0 - 6.0 * half, 1.0 - 6.0 * coupling_full

    def scale(i, _):
        for j in range(arms):
            u = factor(j, i)
            p = u * values(j, i)
            p_ref[j, i] = p
            t_ref[j, i] = u * p

    def inner(i, _):
        for j in range(arms):
            u = factor(j, i)
            p = p_ref[j, i]
            around = beside(p) + (p_ref[j, i - 1] + p_ref[j, i + 1])
            s_ref[j, i] = (u * u) * (centre_half * p + half * around)

    def outer(i, _):
        for j in range(arms):
            u = factor(j, i)
            s, t = s_ref[j, i], t_ref[j, i]
            s_around = beside(s) + (s_ref[j, i - 1] + s_ref[j, i + 1])
            t_around = beside(t) + (t_ref[j, i - 1] + t_ref[j, i + 1])
            halves = (4.0 / 3.0 * centre_half) * s + (4.0 / 3.0 * half) * s_around
            whole = (centre_full / 3.0) * t + (coupling_full / 3.0) * t_around
            store(j, i, u * (halves - u * whole))

    lax.fori_loop(first, last, scale, None)
    lax.fori_loop(first + 1, last - 1, inner, None)
    lax.fori_loop(first + 2, last - 2, outer, None)


def forward_kernel(
    labels, starts, swap, straight, across, fields,
    f_swap, f_straight, f_across, g_swap, g_straight, g_across,
    u_ref, one_ref, low_ref, high_ref, keep_ref, send_ref,
    q_ref, p_ref, t_ref, s_ref, product_ref,
):
    block = starts.shape[1]
    arms = swap.shape[0]
    side = lax.rem(lax.axis_index("space"), 2)
    core = lax.rem(lax.axis_index("arm"), 2)
    own_at, swap_at = block + side * block, 2 * block - side * block
    straight_at, across_at = 3 * block * (1 - side), 3 * block * side

    def gain(field):
        return jnp.exp(field * (-contour_step / 4))

    def fill(i, _):
        for kind in range(2):
            u_ref[kind, own_at + i] = gain(fields[kind, i])
        for at, mine, other in (
            (swap_at, f_swap, g_swap),
            (straight_at, f_straight, g_straight),
            (across_at, f_across, g_across),
        ):
            u_ref[core, at + i] = gain(mine[i])
            u_ref[1 - core, at + i] = gain(other[i])
        for j in range(arms):
            q_ref[j, own_at + i] = starts[side * arms + j, i]
            q_ref[j, swap_at + i] = swap[j, i]
            q_ref[j, straight_at + i] = straight[j, i]
            q_ref[j, across_at + i] = across[j, i]

    lax.fori_loop(0, block, fill, None)
    kinds = [labels[side * arms + j] for j in range(arms)]

    def factor(j, i):
        return u_ref[kinds[j], i]

    def values(j, i):
        return q_ref[j, i]

    def store(j, i, value):
        q_ref[j, i] = value

    inner_at = block - 2 * reach
    contour(inner_at, 4 * block - inner_at, arms, factor, values, store, p_ref, t_ref, s_ref)
    for j in range(arms):
        one_ref[j] = q_ref[j, block : 3 * block]
    inner_at = block - reach
    contour(inner_at, 4 * block - inner_at, arms, factor, values, store, p_ref, t_ref, s_ref)

    def finish(i, _):
        low, high = q_ref[0, block + i], q_ref[0, 2 * block + i]
        low_ref[0, i], high_ref[0, i] = low, high
        for j in range(1, arms):
            low_next, high_next = q_ref[j, block + i], q_ref[j, 2 * block + i]
            low_ref[j, i], high_ref[j, i] = low_next, high_next
            low, high = low * low_next, high * high_next
        product_ref[0, i], product_ref[1, i] = low, high
        keep_ref[i] = product_ref[core, i]
        send_ref[i] = product_ref[1 - core, i]

    lax.fori_loop(0, block, finish, None)


def backward_kernel(
    labels, u_ref, one_ref, two_left, two_low, two_high, two_right,
    j_mine, j_other, j_halo, j_halo_other,
    keep_ref, send_ref,
    junction_ref, q_ref, p_ref, t_ref, s_ref, density_ref,
):
    arms, block = two_low.shape[0], two_low.shape[1]
    side = lax.rem(lax.axis_index("space"), 2)
    core = lax.rem(lax.axis_index("arm"), 2)
    kinds = [labels[side * arms + j] for j in range(arms)]

    def fill(i, _):
        junction_ref[block + core * block + i] = j_mine[i]
        junction_ref[2 * block - core * block + i] = j_other[i]
        junction_ref[3 * block * (1 - core) + i] = j_halo[i]
        junction_ref[3 * block * core + i] = j_halo_other[i]
        for place, two in enumerate((two_left, two_low, two_high, two_right)):
            whole = junction_ref[place * block + i]
            for j in range(arms):
                q_ref[j, place * block + i] = whole / two[j, i]

    lax.fori_loop(0, block, fill, None)

    def factor(j, i):
        return u_ref[kinds[j], i]

    def values(j, i):
        return q_ref[j, i]

    def store(j, i, value):
        q_ref[j, i] = value

    inner_at = block - 2 * reach
    contour(inner_at, 4 * block - inner_at, arms, factor, values, store, p_ref, t_ref, s_ref)
    for j in range(arms):
        one_ref_j = one_ref[j]
        density_ref[j] = 0.5 * one_ref_j * q_ref[j, block : 3 * block]
    inner_at = block - reach
    contour(inner_at, 4 * block - inner_at, arms, factor, values, store, p_ref, t_ref, s_ref)

    is_a = [(kind == 0).astype(jnp.float32) for kind in kinds]

    def segment(i, _):
        quarter = 0.25 * junction_ref[block + i]
        total_a = total_b = None
        for j in range(arms):
            value = density_ref[j, i] + 0.25 * q_ref[j, block + i] + quarter
            part_a, part_b = is_a[j] * value, (1.0 - is_a[j]) * value
            total_a = part_a if j == 0 else total_a + part_a
            total_b = part_b if j == 0 else total_b + part_b
        s_ref[0, i], s_ref[1, i] = total_a, total_b

    lax.fori_loop(0, 2 * block, segment, None)
    chips, owned = keep_ref.shape[0], keep_ref.shape[4]

    def spread(i, _):
        for chip in range(chips):
            mine = pl.ds(pl.multiple_of((2 * chip + core) * owned, 8), owned)
            other = pl.ds(pl.multiple_of((2 * chip + 1 - core) * owned, 8), owned)
            for part in range(2):
                for kind in range(2):
                    keep_ref[chip, part, kind, i] = s_ref[kind, part * block + i, mine]
                    send_ref[chip, part, kind, i] = s_ref[kind, part * block + i, other]

    lax.fori_loop(0, block, spread, None)


def meet_kernel(keep, received, own_ref, *out_refs):
    chips = keep.shape[0]
    side = lax.rem(lax.axis_index("space"), 2)
    chip = lax.div(lax.axis_index("arm"), 2)
    own_ref[...] = keep[chip, side] + received[chip, side]
    for out_ref, (step, flip) in zip(out_refs, other_chips(chips)):
        to_chip = lax.rem(chip + step, chips)
        to_side = 1 - side if flip else side
        out_ref[...] = keep[to_chip, to_side] + received[to_chip, to_side]


def final_kernel(cell_count, arm_count, fields, total, own, *refs):
    *others, density_ref, new_ref = refs
    owned = own.shape[2]
    scale = cell_count / (arm_count * jnp.sum(total[...]))
    rows = pl.ds(pl.multiple_of(lax.axis_index("arm") * owned, 8), owned)
    density = own[...]
    for other in others:
        density = density + other[...]
    density = density * scale
    density_ref[...] = density
    field_a, field_b = fields[0, :, rows], fields[1, :, rows]
    pressure = 0.5 * (field_a + field_b - chi_value)
    new_ref[0] = field_a + mixing * (chi_value * density[1] + pressure - field_a)
    new_ref[1] = field_b + mixing * (chi_value * density[0] + pressure - field_b)


def other_chips(chips):
    return [(step, flip) for step in range(chips) for flip in (False, True) if step or flip]


def vmem(shape):
    return pltpu.VMEM(shape, jnp.float32)


def f32(shape):
    return jax.ShapeDtypeStruct(shape, jnp.float32)


def call(kernel, out_shape, scratch, smem, *args, cost=1_000_000):
    specs = [pl.BlockSpec(memory_space=pltpu.SMEM if k < smem else pltpu.VMEM) for k in range(len(args))]
    return pl.pallas_call(
        kernel,
        out_shape=out_shape,
        in_specs=specs,
        out_specs=jax.tree.map(lambda _: pl.BlockSpec(memory_space=pltpu.VMEM), out_shape),
        scratch_shapes=scratch,
        compiler_params=pltpu.CompilerParams(vmem_limit_bytes=40 * 1024 * 1024),
        cost_estimate=pl.CostEstimate(flops=cost, bytes_accessed=cost, transcendentals=0),
    )(*args)


def local(fields, starts, labels):
    arm_size, space_size = lax.axis_size("arm"), lax.axis_size("space")
    chips, pairs = arm_size // 2, space_size // 2
    held, block, rows, columns = starts.shape
    arms = held // 2
    owned = rows // arm_size
    side = lax.rem(lax.axis_index("space"), 2)
    core = lax.rem(lax.axis_index("arm"), 2)

    def send(value, target):
        perm = []
        for a in range(arm_size):
            for s in range(space_size):
                chip_to, core_to, pair_to, side_to = target(a // 2, a % 2, s // 2, s % 2)
                to = (2 * (chip_to % chips) + core_to) * space_size + 2 * (pair_to % pairs) + side_to
                perm.append((a * space_size + s, to))
        return lax.ppermute(value, AXES, perm)

    def to_core(value):
        return send(value, lambda x, c, p, h: (x, 1 - c, p, h))

    def to_side(value):
        return send(value, lambda x, c, p, h: (x, c, p, 1 - h))

    def to_straight(value):
        return send(value, lambda x, c, p, h: (x, c, p + 2 * h - 1, h))

    def to_across(value):
        return send(value, lambda x, c, p, h: (x, c, p + 2 * h - 1, 1 - h))

    field_own = lax.dynamic_index_in_dim(fields, core, 0, keepdims=False)
    field_got = [to_side(field_own), to_straight(field_own), to_across(field_own)]
    start_own = lax.dynamic_slice_in_dim(starts, side * arms, arms, 0)
    start_other = lax.dynamic_slice_in_dim(starts, (1 - side) * arms, arms, 0)
    start_got = [to_side(start_other), to_straight(start_own), to_across(start_other)]
    field_more = [to_core(value) for value in field_got]

    wide = vmem((arms, 4 * block, rows, columns))
    whole = (arms, 2 * block, rows, columns)
    part = (arms, block, rows, columns)
    one = (block, rows, columns)
    factor, step_one, low, high, keep, give = call(
        forward_kernel,
        (f32((2, 4 * block, rows, columns)), f32(whole), f32(part), f32(part), f32(one), f32(one)),
        [wide, wide, wide, wide, vmem((2,) + one)],
        1,
        labels, starts, *start_got, fields, *field_got, *field_more,
        cost=8_000_000,
    )
    right = send(low, lambda x, c, p, h: (x, c, p - 1, h))
    left = send(high, lambda x, c, p, h: (x, c, p + 1, h))
    mine = keep * to_core(give)
    junction = mine
    for step, flip in other_chips(chips):
        junction = junction * send(
            mine, lambda x, c, p, h, step=step, flip=flip: (x + step, c, p, 1 - h if flip else h)
        )
    junction_other = to_core(junction)
    halo = send(junction, lambda x, c, p, h: (x, c, p + 2 * c - 1, h))
    halo_other = to_core(halo)

    total = jnp.sum(junction.reshape(-1, 8, columns), axis=0)
    total = total + to_core(total)
    if pairs & (pairs - 1) == 0:
        step = 1
        while step < pairs:
            total = total + send(total, lambda x, c, p, h, step=step: (x, c, p + step, h))
            step *= 2
    else:
        total = lax.psum(total, "space") / 2.0

    parts = (chips, 2, 2, block, owned, columns)
    keep, give = call(
        backward_kernel,
        (f32(parts), f32(parts)),
        [vmem((4 * block, rows, columns)), wide, wide, wide, wide, vmem(whole)],
        1,
        labels, factor, step_one, left, low, high, right, junction, junction_other, halo, halo_other,
        cost=8_000_000,
    )
    places = other_chips(chips)
    own, *gives = call(
        meet_kernel, (f32(parts[2:]),) * (1 + len(places)), [], 0, keep, to_core(give)
    )
    received = [
        send(value, lambda x, c, p, h, step=step, flip=flip: (x + step, c, p, 1 - h if flip else h))
        for value, (step, flip) in zip(gives, places)
    ]
    cell_count = block * space_size * rows * columns
    return call(
        functools.partial(final_kernel, cell_count, held * arm_size),
        (f32(parts[2:]), f32(parts[2:])),
        [],
        0,
        fields, total, own, *received,
    )


def solution(mesh):
    in_specs = (P(None, "space", None, None), P("arm", "space", None, None), P("arm"))
    out_specs = (P(None, "space", "arm", None), P(None, "space", "arm", None))
    return jax.shard_map(local, mesh=mesh, in_specs=in_specs, out_specs=out_specs, check_vma=False)
```

```python
import functools

import jax
import jax.numpy as jnp
from jax import lax
from jax.experimental import pallas as pl
from jax.experimental.pallas import tpu as pltpu
from jax.sharding import PartitionSpec as P

coupling_full = 0.15
contour_step = 0.05
chi_value = 2.0
mixing = 0.5
reach = 2

AXES = ("arm", "space")


def beside(plane):
    rows, columns = plane.shape
    total = pltpu.roll(plane, 1, 0) + pltpu.roll(plane, rows - 1, 0)
    return total + (pltpu.roll(plane, 1, 1) + pltpu.roll(plane, columns - 1, 1))


def contour(first, last, arms, factor, values, store, p_ref, t_ref, s_ref):
    half = coupling_full / 2
    centre_half, centre_full = 1.0 - 6.0 * half, 1.0 - 6.0 * coupling_full

    def scale(i, _):
        for j in range(arms):
            u = factor(j, i)
            p = u * values(j, i)
            p_ref[j, i] = p
            t_ref[j, i] = u * p

    def inner(i, _):
        for j in range(arms):
            u = factor(j, i)
            p = p_ref[j, i]
            around = beside(p) + (p_ref[j, i - 1] + p_ref[j, i + 1])
            s_ref[j, i] = (u * u) * (centre_half * p + half * around)

    def outer(i, _):
        for j in range(arms):
            u = factor(j, i)
            s, t = s_ref[j, i], t_ref[j, i]
            s_around = beside(s) + (s_ref[j, i - 1] + s_ref[j, i + 1])
            t_around = beside(t) + (t_ref[j, i - 1] + t_ref[j, i + 1])
            halves = (4.0 / 3.0 * centre_half) * s + (4.0 / 3.0 * half) * s_around
            whole = (centre_full / 3.0) * t + (coupling_full / 3.0) * t_around
            store(j, i, u * (halves - u * whole))

    lax.fori_loop(first, last, scale, None, unroll=4)
    lax.fori_loop(first + 1, last - 1, inner, None, unroll=4)
    lax.fori_loop(first + 2, last - 2, outer, None, unroll=4)


def pack_kernel(starts, fields, own_ref, other_ref, sems):
    arms = starts.shape[0] // 2
    side = lax.rem(lax.axis_index("space"), 2)
    core = lax.rem(lax.axis_index("arm"), 2)
    copies = []
    for k, (out_ref, at) in enumerate(((other_ref, 1 - side), (own_ref, side))):
        copies.append(
            pltpu.make_async_copy(starts.at[pl.ds(at * arms, arms)], out_ref.at[pl.ds(0, arms)], sems.at[2 * k])
        )
        copies.append(pltpu.make_async_copy(fields.at[core], out_ref.at[arms], sems.at[2 * k + 1]))
    for copy in copies:
        copy.start()
    for copy in copies:
        copy.wait()


def forward_kernel(
    labels, starts, fields, swap, straight, across, g_swap, g_straight, g_across,
    u_ref, one_ref, low_ref, high_ref, keep_ref, send_ref,
    q_ref, p_ref, t_ref, s_ref, product_ref,
):
    block = starts.shape[1]
    arms = starts.shape[0] // 2
    side = lax.rem(lax.axis_index("space"), 2)
    core = lax.rem(lax.axis_index("arm"), 2)
    own_at, swap_at = block + side * block, 2 * block - side * block
    straight_at, across_at = 3 * block * (1 - side), 3 * block * side

    def gain(field):
        return jnp.exp(field * (-contour_step / 4))

    def fill(i, _):
        for kind in range(2):
            u_ref[kind, own_at + i] = gain(fields[kind, i])
        for at, mine, other in (
            (swap_at, swap, g_swap),
            (straight_at, straight, g_straight),
            (across_at, across, g_across),
        ):
            u_ref[core, at + i] = gain(mine[arms, i])
            u_ref[1 - core, at + i] = gain(other[arms, i])
        for j in range(arms):
            q_ref[j, own_at + i] = starts[side * arms + j, i]
            q_ref[j, swap_at + i] = swap[j, i]
            q_ref[j, straight_at + i] = straight[j, i]
            q_ref[j, across_at + i] = across[j, i]

    lax.fori_loop(0, block, fill, None)
    kinds = [labels[side * arms + j] for j in range(arms)]

    def factor(j, i):
        return u_ref[kinds[j], i]

    def values(j, i):
        return q_ref[j, i]

    def store(j, i, value):
        q_ref[j, i] = value

    inner_at = block - 2 * reach
    contour(inner_at, 4 * block - inner_at, arms, factor, values, store, p_ref, t_ref, s_ref)
    for j in range(arms):
        one_ref[j] = q_ref[j, block : 3 * block]
    inner_at = block - reach
    contour(inner_at, 4 * block - inner_at, arms, factor, values, store, p_ref, t_ref, s_ref)

    def finish(i, _):
        low, high = q_ref[0, block + i], q_ref[0, 2 * block + i]
        low_ref[0, i], high_ref[0, i] = low, high
        for j in range(1, arms):
            low_next, high_next = q_ref[j, block + i], q_ref[j, 2 * block + i]
            low_ref[j, i], high_ref[j, i] = low_next, high_next
            low, high = low * low_next, high * high_next
        product_ref[0, i], product_ref[1, i] = low, high
        keep_ref[i] = product_ref[core, i]
        send_ref[i] = product_ref[1 - core, i]

    lax.fori_loop(0, block, finish, None)


def backward_kernel(
    labels, u_ref, one_ref, two_left, two_low, two_high, two_right,
    j_mine, j_other, j_halo, j_halo_other,
    keep_ref, send_ref, total_ref,
    junction_ref, q_ref, p_ref, t_ref, s_ref, density_ref,
):
    arms, block = two_low.shape[0], two_low.shape[1]
    side = lax.rem(lax.axis_index("space"), 2)
    core = lax.rem(lax.axis_index("arm"), 2)
    kinds = [labels[side * arms + j] for j in range(arms)]

    total_ref[...] = jnp.zeros_like(total_ref)

    def fill(i, _):
        junction_ref[block + core * block + i] = j_mine[i]
        junction_ref[2 * block - core * block + i] = j_other[i]
        junction_ref[3 * block * (1 - core) + i] = j_halo[i]
        junction_ref[3 * block * core + i] = j_halo_other[i]
        for place, two in enumerate((two_left, two_low, two_high, two_right)):
            whole = junction_ref[place * block + i]
            total_ref[...] += jnp.sum(whole.reshape(-1, *total_ref.shape), axis=0)
            for j in range(arms):
                q_ref[j, place * block + i] = whole / two[j, i]

    lax.fori_loop(0, block, fill, None)

    def factor(j, i):
        return u_ref[kinds[j], i]

    def values(j, i):
        return q_ref[j, i]

    def store(j, i, value):
        q_ref[j, i] = value

    inner_at = block - 2 * reach
    contour(inner_at, 4 * block - inner_at, arms, factor, values, store, p_ref, t_ref, s_ref)
    for j in range(arms):
        one_ref_j = one_ref[j]
        density_ref[j] = 0.5 * one_ref_j * q_ref[j, block : 3 * block]
    inner_at = block - reach
    contour(inner_at, 4 * block - inner_at, arms, factor, values, store, p_ref, t_ref, s_ref)

    is_a = [(kind == 0).astype(jnp.float32) for kind in kinds]

    def segment(i, _):
        quarter = 0.25 * junction_ref[block + i]
        total_a = total_b = None
        for j in range(arms):
            value = density_ref[j, i] + 0.25 * q_ref[j, block + i] + quarter
            part_a, part_b = is_a[j] * value, (1.0 - is_a[j]) * value
            total_a = part_a if j == 0 else total_a + part_a
            total_b = part_b if j == 0 else total_b + part_b
        s_ref[0, i], s_ref[1, i] = total_a, total_b

    lax.fori_loop(0, 2 * block, segment, None)
    chips, owned = keep_ref.shape[0], keep_ref.shape[4]

    def spread(i, _):
        for chip in range(chips):
            mine = pl.ds(pl.multiple_of((2 * chip + core) * owned, 8), owned)
            other = pl.ds(pl.multiple_of((2 * chip + 1 - core) * owned, 8), owned)
            for part in range(2):
                for kind in range(2):
                    keep_ref[chip, part, kind, i] = s_ref[kind, part * block + i, mine]
                    send_ref[chip, part, kind, i] = s_ref[kind, part * block + i, other]

    lax.fori_loop(0, block, spread, None)


def meet_kernel(keep, received, own_ref, *out_refs):
    chips = keep.shape[0]
    side = lax.rem(lax.axis_index("space"), 2)
    chip = lax.div(lax.axis_index("arm"), 2)
    own_ref[...] = keep[chip, side] + received[chip, side]
    for out_ref, (step, flip) in zip(out_refs, other_chips(chips)):
        to_chip = lax.rem(chip + step, chips)
        to_side = 1 - side if flip else side
        out_ref[...] = keep[to_chip, to_side] + received[to_chip, to_side]


def final_kernel(cell_count, arm_count, fields, total, own, *refs):
    *others, density_ref, new_ref = refs
    owned = own.shape[2]
    scale = cell_count / (arm_count * jnp.sum(total[...]))
    rows = pl.ds(pl.multiple_of(lax.axis_index("arm") * owned, 8), owned)
    density = own[...]
    for other in others:
        density = density + other[...]
    density = density * scale
    density_ref[...] = density
    field_a, field_b = fields[0, :, rows], fields[1, :, rows]
    pressure = 0.5 * (field_a + field_b - chi_value)
    new_ref[0] = field_a + mixing * (chi_value * density[1] + pressure - field_a)
    new_ref[1] = field_b + mixing * (chi_value * density[0] + pressure - field_b)


def other_chips(chips):
    return [(step, flip) for step in range(chips) for flip in (False, True) if step or flip]


def vmem(shape):
    return pltpu.VMEM(shape, jnp.float32)


def f32(shape):
    return jax.ShapeDtypeStruct(shape, jnp.float32)


def call(kernel, out_shape, scratch, smem, *args, cost=1_000_000):
    specs = [pl.BlockSpec(memory_space=pltpu.SMEM if k < smem else pltpu.VMEM) for k in range(len(args))]
    return pl.pallas_call(
        kernel,
        out_shape=out_shape,
        in_specs=specs,
        out_specs=jax.tree.map(lambda _: pl.BlockSpec(memory_space=pltpu.VMEM), out_shape),
        scratch_shapes=scratch,
        compiler_params=pltpu.CompilerParams(vmem_limit_bytes=40 * 1024 * 1024),
        cost_estimate=pl.CostEstimate(flops=cost, bytes_accessed=cost, transcendentals=0),
    )(*args)


def local(fields, starts, labels):
    arm_size, space_size = lax.axis_size("arm"), lax.axis_size("space")
    chips, pairs = arm_size // 2, space_size // 2
    held, block, rows, columns = starts.shape
    arms = held // 2
    owned = rows // arm_size
    side = lax.rem(lax.axis_index("space"), 2)
    core = lax.rem(lax.axis_index("arm"), 2)

    def send(value, target):
        perm = []
        for a in range(arm_size):
            for s in range(space_size):
                chip_to, core_to, pair_to, side_to = target(a // 2, a % 2, s // 2, s % 2)
                to = (2 * (chip_to % chips) + core_to) * space_size + 2 * (pair_to % pairs) + side_to
                perm.append((a * space_size + s, to))
        return lax.ppermute(value, AXES, perm)

    def to_core(value):
        return send(value, lambda x, c, p, h: (x, 1 - c, p, h))

    def to_side(value):
        return send(value, lambda x, c, p, h: (x, c, p, 1 - h))

    def to_straight(value):
        return send(value, lambda x, c, p, h: (x, c, p + 2 * h - 1, h))

    def to_across(value):
        return send(value, lambda x, c, p, h: (x, c, p + 2 * h - 1, 1 - h))

    message = f32((arms + 1, block, rows, columns))
    own_set, other_set = pl.pallas_call(
        pack_kernel,
        out_shape=(message, message),
        in_specs=[pl.BlockSpec(memory_space=pl.ANY)] * 2,
        out_specs=[pl.BlockSpec(memory_space=pltpu.VMEM)] * 2,
        scratch_shapes=[pltpu.SemaphoreType.DMA((4,))],
    )(starts, fields)
    across = to_across(other_set)
    swap = to_side(other_set)
    straight = to_straight(own_set)
    got = [swap, straight, across]
    got_more = [to_core(value) for value in got]

    wide = vmem((arms, 4 * block, rows, columns))
    whole = (arms, 2 * block, rows, columns)
    part = (arms, block, rows, columns)
    one = (block, rows, columns)
    factor, step_one, low, high, keep, give = call(
        forward_kernel,
        (f32((2, 4 * block, rows, columns)), f32(whole), f32(part), f32(part), f32(one), f32(one)),
        [wide, wide, wide, wide, vmem((2,) + one)],
        1,
        labels, starts, fields, *got, *got_more,
        cost=8_000_000,
    )
    right = send(low, lambda x, c, p, h: (x, c, p - 1, h))
    left = send(high, lambda x, c, p, h: (x, c, p + 1, h))
    mine = keep * to_core(give)
    junction = mine
    for step, flip in other_chips(chips):
        junction = junction * send(
            mine, lambda x, c, p, h, step=step, flip=flip: (x + step, c, p, 1 - h if flip else h)
        )
    halo = send(junction, lambda x, c, p, h: (x, c, p + 2 * c - 1, h))
    held_junction, left, right = lax.optimization_barrier((junction, left, right))
    junction_other = to_core(held_junction)
    halo_other = to_core(halo)

    parts = (chips, 2, 2, block, owned, columns)
    keep, give, total = call(
        backward_kernel,
        (f32(parts), f32(parts), f32((8, columns))),
        [vmem((4 * block, rows, columns)), wide, wide, wide, wide, vmem(whole)],
        1,
        labels, factor, step_one, left, low, high, right, junction, junction_other, halo, halo_other,
        cost=8_000_000,
    )
    if pairs & (pairs - 1) == 0:
        step = 2
        while step < pairs:
            total = total + send(total, lambda x, c, p, h, step=step: (x, c, p + step, h))
            step *= 2
    else:
        total = lax.psum(total, "space") / 4.0
    places = other_chips(chips)
    own, *gives = call(
        meet_kernel, (f32(parts[2:]),) * (1 + len(places)), [], 0, keep, to_core(give)
    )
    received = [
        send(value, lambda x, c, p, h, step=step, flip=flip: (x + step, c, p, 1 - h if flip else h))
        for value, (step, flip) in zip(gives, places)
    ]
    cell_count = block * space_size * rows * columns
    return call(
        functools.partial(final_kernel, cell_count, held * arm_size),
        (f32(parts[2:]), f32(parts[2:])),
        [],
        0,
        fields, total, own, *received,
    )


def solution(mesh):
    in_specs = (P(None, "space", None, None), P("arm", "space", None, None), P("arm"))
    out_specs = (P(None, "space", "arm", None), P(None, "space", "arm", None))
    return jax.shard_map(local, mesh=mesh, in_specs=in_specs, out_specs=out_specs, check_vma=False)
```

```python
import functools

import jax
import jax.numpy as jnp
from jax import lax
from jax.experimental import pallas as pl
from jax.experimental.pallas import tpu as pltpu
from jax.sharding import PartitionSpec as P

coupling_full = 0.15
contour_step = 0.05
chi_value = 2.0
mixing = 0.5
reach = 2

AXES = ("arm", "space")


def beside(plane):
    rows, columns = plane.shape
    total = pltpu.roll(plane, 1, 0) + pltpu.roll(plane, rows - 1, 0)
    return total + (pltpu.roll(plane, 1, 1) + pltpu.roll(plane, columns - 1, 1))


def contour(first, last, arms, factor, values, store, p_ref, t_ref, s_ref):
    half = coupling_full / 2
    centre_half, centre_full = 1.0 - 6.0 * half, 1.0 - 6.0 * coupling_full

    def scale(i, _):
        for j in range(arms):
            u = factor(j, i)
            p = u * values(j, i)
            p_ref[j, i] = p
            t_ref[j, i] = u * p

    def inner(i, _):
        for j in range(arms):
            u = factor(j, i)
            p = p_ref[j, i]
            around = beside(p) + (p_ref[j, i - 1] + p_ref[j, i + 1])
            s_ref[j, i] = (u * u) * (centre_half * p + half * around)

    def outer(i, _):
        for j in range(arms):
            u = factor(j, i)
            s, t = s_ref[j, i], t_ref[j, i]
            s_around = beside(s) + (s_ref[j, i - 1] + s_ref[j, i + 1])
            t_around = beside(t) + (t_ref[j, i - 1] + t_ref[j, i + 1])
            halves = (4.0 / 3.0 * centre_half) * s + (4.0 / 3.0 * half) * s_around
            whole = (centre_full / 3.0) * t + (coupling_full / 3.0) * t_around
            store(j, i, u * (halves - u * whole))

    lax.fori_loop(first, last, scale, None, unroll=4)
    lax.fori_loop(first + 1, last - 1, inner, None, unroll=4)
    lax.fori_loop(first + 2, last - 2, outer, None, unroll=4)


def pack_kernel(starts, fields, field_ref, other_ref, own_ref, sems):
    arms = starts.shape[0] // 2
    side = lax.rem(lax.axis_index("space"), 2)
    core = lax.rem(lax.axis_index("arm"), 2)
    copies = [
        pltpu.make_async_copy(fields.at[core], field_ref, sems.at[0]),
        pltpu.make_async_copy(starts.at[pl.ds((1 - side) * arms, arms)], other_ref, sems.at[1]),
        pltpu.make_async_copy(starts.at[pl.ds(side * arms, arms)], own_ref, sems.at[2]),
    ]
    for copy in copies:
        copy.start()
    for copy in copies:
        copy.wait()


def places(block):
    side = lax.rem(lax.axis_index("space"), 2)
    return block + side * block, 2 * block - side * block, 3 * block * (1 - side), 3 * block * side


def window_kernel(starts, across, out_ref):
    arms = across.shape[0]
    side = lax.rem(lax.axis_index("space"), 2)
    for j in range(arms):
        out_ref[j] = starts[side * arms + j]
        out_ref[arms + j] = across[j]


def forward_kernel(
    labels, window, swap, straight, fields, f_straight, g_straight, piece, piece_core, piece_chip, piece_both,
    u_ref, one_ref, low_ref, high_ref, keep_ref, send_ref,
    q_ref, p_ref, t_ref, s_ref, product_ref,
):
    block = fields.shape[1]
    arms = swap.shape[0]
    side = lax.rem(lax.axis_index("space"), 2)
    core = lax.rem(lax.axis_index("arm"), 2)
    own_at, swap_at, straight_at, across_at = places(block)
    chip = lax.div(lax.axis_index("arm"), 2)
    here_at = swap_at + chip * (across_at - swap_at)
    there_at = across_at + chip * (swap_at - across_at)

    def gain(field):
        return jnp.exp(field * (-contour_step / 4))

    def fill(i, _):
        for kind in range(2):
            u_ref[kind, own_at + i] = gain(fields[kind, i])
        u_ref[core, here_at + i] = gain(piece[i])
        u_ref[1 - core, here_at + i] = gain(piece_core[i])
        u_ref[core, there_at + i] = gain(piece_chip[i])
        u_ref[1 - core, there_at + i] = gain(piece_both[i])
        u_ref[core, straight_at + i] = gain(f_straight[i])
        u_ref[1 - core, straight_at + i] = gain(g_straight[i])
        for j in range(arms):
            q_ref[j, own_at + i] = window[j, i]
            q_ref[j, across_at + i] = window[arms + j, i]
            q_ref[j, swap_at + i] = swap[j, i]
            q_ref[j, straight_at + i] = straight[j, i]

    lax.fori_loop(0, block, fill, None)
    kinds = [labels[side * arms + j] for j in range(arms)]

    def factor(j, i):
        return u_ref[kinds[j], i]

    def values(j, i):
        return q_ref[j, i]

    def store(j, i, value):
        q_ref[j, i] = value

    inner_at = block - 2 * reach
    contour(inner_at, 4 * block - inner_at, arms, factor, values, store, p_ref, t_ref, s_ref)
    for j in range(arms):
        one_ref[j] = q_ref[j, block : 3 * block]
    inner_at = block - reach
    contour(inner_at, 4 * block - inner_at, arms, factor, values, store, p_ref, t_ref, s_ref)

    def finish(i, _):
        low, high = q_ref[0, block + i], q_ref[0, 2 * block + i]
        low_ref[0, i], high_ref[0, i] = low, high
        for j in range(1, arms):
            low_next, high_next = q_ref[j, block + i], q_ref[j, 2 * block + i]
            low_ref[j, i], high_ref[j, i] = low_next, high_next
            low, high = low * low_next, high * high_next
        product_ref[0, i], product_ref[1, i] = low, high
        keep_ref[i] = product_ref[core, i]
        send_ref[i] = product_ref[1 - core, i]

    lax.fori_loop(0, block, finish, None)


def backward_kernel(
    labels, u_ref, one_ref, two_left, two_low, two_high, two_right,
    j_mine, j_other, j_halo, j_halo_other,
    keep_ref, send_ref, total_ref,
    junction_ref, q_ref, p_ref, t_ref, s_ref, density_ref,
):
    arms, block = two_low.shape[0], two_low.shape[1]
    side = lax.rem(lax.axis_index("space"), 2)
    core = lax.rem(lax.axis_index("arm"), 2)
    kinds = [labels[side * arms + j] for j in range(arms)]

    total_ref[...] = jnp.zeros_like(total_ref)

    def fill(i, _):
        junction_ref[block + core * block + i] = j_mine[i]
        junction_ref[2 * block - core * block + i] = j_other[i]
        junction_ref[3 * block * (1 - core) + i] = j_halo[i]
        junction_ref[3 * block * core + i] = j_halo_other[i]
        for place, two in enumerate((two_left, two_low, two_high, two_right)):
            whole = junction_ref[place * block + i]
            total_ref[...] += jnp.sum(whole.reshape(-1, *total_ref.shape), axis=0)
            for j in range(arms):
                q_ref[j, place * block + i] = whole / two[j, i]

    lax.fori_loop(0, block, fill, None)

    def factor(j, i):
        return u_ref[kinds[j], i]

    def values(j, i):
        return q_ref[j, i]

    def store(j, i, value):
        q_ref[j, i] = value

    inner_at = block - 2 * reach
    contour(inner_at, 4 * block - inner_at, arms, factor, values, store, p_ref, t_ref, s_ref)
    for j in range(arms):
        one_ref_j = one_ref[j]
        density_ref[j] = 0.5 * one_ref_j * q_ref[j, block : 3 * block]
    inner_at = block - reach
    contour(inner_at, 4 * block - inner_at, arms, factor, values, store, p_ref, t_ref, s_ref)

    is_a = [(kind == 0).astype(jnp.float32) for kind in kinds]

    def segment(i, _):
        quarter = 0.25 * junction_ref[block + i]
        total_a = total_b = None
        for j in range(arms):
            value = density_ref[j, i] + 0.25 * q_ref[j, block + i] + quarter
            part_a, part_b = is_a[j] * value, (1.0 - is_a[j]) * value
            total_a = part_a if j == 0 else total_a + part_a
            total_b = part_b if j == 0 else total_b + part_b
        s_ref[0, i], s_ref[1, i] = total_a, total_b

    lax.fori_loop(0, 2 * block, segment, None)
    chips, owned = keep_ref.shape[0], keep_ref.shape[4]

    def spread(i, _):
        for chip in range(chips):
            mine = pl.ds(pl.multiple_of((2 * chip + core) * owned, 8), owned)
            other = pl.ds(pl.multiple_of((2 * chip + 1 - core) * owned, 8), owned)
            for part in range(2):
                for kind in range(2):
                    keep_ref[chip, part, kind, i] = s_ref[kind, part * block + i, mine]
                    send_ref[chip, part, kind, i] = s_ref[kind, part * block + i, other]

    lax.fori_loop(0, block, spread, None)


def meet_kernel(keep, received, own_ref, *out_refs):
    chips = keep.shape[0]
    side = lax.rem(lax.axis_index("space"), 2)
    chip = lax.div(lax.axis_index("arm"), 2)
    own_ref[...] = keep[chip, side] + received[chip, side]
    for out_ref, (step, flip) in zip(out_refs, other_chips(chips)):
        to_chip = lax.rem(chip + step, chips)
        to_side = 1 - side if flip else side
        out_ref[...] = keep[to_chip, to_side] + received[to_chip, to_side]


def final_kernel(cell_count, arm_count, fields, total, own, *refs):
    *others, density_ref, new_ref = refs
    owned = own.shape[2]
    scale = cell_count / (arm_count * jnp.sum(total[...]))
    rows = pl.ds(pl.multiple_of(lax.axis_index("arm") * owned, 8), owned)
    density = own[...]
    for other in others:
        density = density + other[...]
    density = density * scale
    density_ref[...] = density
    field_a, field_b = fields[0, :, rows], fields[1, :, rows]
    pressure = 0.5 * (field_a + field_b - chi_value)
    new_ref[0] = field_a + mixing * (chi_value * density[1] + pressure - field_a)
    new_ref[1] = field_b + mixing * (chi_value * density[0] + pressure - field_b)


def other_chips(chips):
    return [(step, flip) for step in range(chips) for flip in (False, True) if step or flip]


def vmem(shape):
    return pltpu.VMEM(shape, jnp.float32)


def f32(shape):
    return jax.ShapeDtypeStruct(shape, jnp.float32)


def call(kernel, out_shape, scratch, smem, *args, cost=1_000_000):
    specs = [pl.BlockSpec(memory_space=pltpu.SMEM if k < smem else pltpu.VMEM) for k in range(len(args))]
    return pl.pallas_call(
        kernel,
        out_shape=out_shape,
        in_specs=specs,
        out_specs=jax.tree.map(lambda _: pl.BlockSpec(memory_space=pltpu.VMEM), out_shape),
        scratch_shapes=scratch,
        compiler_params=pltpu.CompilerParams(vmem_limit_bytes=40 * 1024 * 1024),
        cost_estimate=pl.CostEstimate(flops=cost, bytes_accessed=cost, transcendentals=0),
    )(*args)


def local(fields, starts, labels):
    arm_size, space_size = lax.axis_size("arm"), lax.axis_size("space")
    chips, pairs = arm_size // 2, space_size // 2
    held, block, rows, columns = starts.shape
    arms = held // 2
    owned = rows // arm_size
    if chips != 2 or held % 2 or space_size % 2:
        raise ValueError("unsupported mesh")
    side = lax.rem(lax.axis_index("space"), 2)
    core = lax.rem(lax.axis_index("arm"), 2)

    def send(value, target):
        perm = []
        for a in range(arm_size):
            for s in range(space_size):
                chip_to, core_to, pair_to, side_to = target(a // 2, a % 2, s // 2, s % 2)
                to = (2 * (chip_to % chips) + core_to) * space_size + 2 * (pair_to % pairs) + side_to
                perm.append((a * space_size + s, to))
        return lax.ppermute(value, AXES, perm)

    def to_core(value):
        return send(value, lambda x, c, p, h: (x, 1 - c, p, h))

    def to_side(value):
        return send(value, lambda x, c, p, h: (x, c, p, 1 - h))

    def to_straight(value):
        return send(value, lambda x, c, p, h: (x, c, p + 2 * h - 1, h))

    def to_across(value):
        return send(value, lambda x, c, p, h: (x, c, p + 2 * h - 1, 1 - h))

    field_own, other_set, own_set = pl.pallas_call(
        pack_kernel,
        out_shape=(
            f32((block, rows, columns)),
            f32((arms, block, rows, columns)),
            f32((arms, block, rows, columns)),
        ),
        in_specs=[pl.BlockSpec(memory_space=pl.ANY)] * 2,
        out_specs=[pl.BlockSpec(memory_space=pltpu.VMEM)] * 3,
        scratch_shapes=[pltpu.SemaphoreType.DMA((3,))],
    )(starts, fields)
    field_got = send(field_own, lambda x, c, p, h: (x, c, p + 2 * h - 1 if x else p, 1 - h))
    across = to_across(other_set)
    swap = to_side(other_set)
    straight = to_straight(own_set)
    pieces = [
        field_got,
        to_core(field_got),
        send(field_got, lambda x, c, p, h: (1 - x, c, p, h)),
        send(field_got, lambda x, c, p, h: (1 - x, 1 - c, p, h)),
    ]
    field_straight = to_straight(field_own)
    straight_more = to_core(field_straight)

    wide = vmem((arms, 4 * block, rows, columns))
    whole = (arms, 2 * block, rows, columns)
    part = (arms, block, rows, columns)
    one = (block, rows, columns)
    window = call(window_kernel, f32((2 * arms, block, rows, columns)), [], 0, starts, across)
    factor, step_one, low, high, keep, give = call(
        forward_kernel,
        (f32((2, 4 * block, rows, columns)), f32(whole), f32(part), f32(part), f32(one), f32(one)),
        [wide, wide, wide, wide, vmem((2,) + one)],
        1,
        labels, window, swap, straight, fields, field_straight, straight_more, *pieces,
        cost=8_000_000,
    )
    right = send(low, lambda x, c, p, h: (x, c, p - 1, h))
    left = send(high, lambda x, c, p, h: (x, c, p + 1, h))
    mine = keep * to_core(give)
    mine = mine * to_side(mine)
    junction = mine
    for step in range(1, chips):
        junction = junction * send(mine, lambda x, c, p, h, step=step: (x + step, c, p, h))
    halo = send(junction, lambda x, c, p, h: (x, c, p + 2 * c - 1, h))
    held_junction, left, right = lax.optimization_barrier((junction, left, right))
    junction_other = to_core(held_junction)
    halo_other = to_core(halo)

    parts = (chips, 2, 2, block, owned, columns)
    keep, give, total = call(
        backward_kernel,
        (f32(parts), f32(parts), f32((8, columns))),
        [vmem((4 * block, rows, columns)), wide, wide, wide, wide, vmem(whole)],
        1,
        labels, factor, step_one, left, low, high, right, junction, junction_other, halo, halo_other,
        cost=8_000_000,
    )
    if pairs & (pairs - 1) == 0:
        step = 2
        while step < pairs:
            total = total + send(total, lambda x, c, p, h, step=step: (x, c, p + step, h))
            step *= 2
    else:
        total = lax.psum(total, "space") / 4.0
    to_places = other_chips(chips)
    own, *gives = call(
        meet_kernel, (f32(parts[2:]),) * (1 + len(to_places)), [], 0, keep, to_core(give)
    )
    received = [
        send(value, lambda x, c, p, h, step=step, flip=flip: (x + step, c, p, 1 - h if flip else h))
        for value, (step, flip) in zip(gives, to_places)
    ]
    cell_count = block * space_size * rows * columns
    return call(
        functools.partial(final_kernel, cell_count, held * arm_size),
        (f32(parts[2:]), f32(parts[2:])),
        [],
        0,
        fields, total, own, *received,
    )


def solution(mesh):
    in_specs = (P(None, "space", None, None), P("arm", "space", None, None), P("arm"))
    out_specs = (P(None, "space", "arm", None), P(None, "space", "arm", None))
    return jax.shard_map(local, mesh=mesh, in_specs=in_specs, out_specs=out_specs, check_vma=False)
```

```python
import functools

import jax
import jax.numpy as jnp
from jax import lax
from jax.experimental import pallas as pl
from jax.experimental.pallas import tpu as pltpu
from jax.sharding import PartitionSpec as P

coupling_full = 0.15
contour_step = 0.05
chi_value = 2.0
mixing = 0.5
reach = 2

AXES = ("arm", "space")


def beside(plane):
    rows, columns = plane.shape
    total = pltpu.roll(plane, 1, 0) + pltpu.roll(plane, rows - 1, 0)
    return total + (pltpu.roll(plane, 1, 1) + pltpu.roll(plane, columns - 1, 1))


def wavefront(stages):
    runs = [(first + 2 * k, last + 2 * k, 2 * k, work) for k, (first, last, work) in enumerate(stages)]
    cuts = sorted({edge for first, last, _, _ in runs for edge in (first, last)})
    for begin, end in zip(cuts, cuts[1:]):
        active = [(lag, work) for first, last, lag, work in runs if first <= begin and end <= last]

        def body(i, _, active=active):
            for lag, work in reversed(active):
                work(i - lag)

        lax.fori_loop(begin, end, body, None)


def two_steps(block, arms, factor, values, middle, store, scratch):
    half = coupling_full / 2
    centre_half, centre_full = 1.0 - 6.0 * half, 1.0 - 6.0 * coupling_full

    def enter(j, i, value, p_ref, t_ref):
        u = factor(j, i)
        p = u * value
        p_ref[j, i] = p
        t_ref[j, i] = u * p

    def inner(i, p_ref, s_ref):
        for j in range(arms):
            u = factor(j, i)
            p = p_ref[j, i]
            around = beside(p) + (p_ref[j, i - 1] + p_ref[j, i + 1])
            s_ref[j, i] = (u * u) * (centre_half * p + half * around)

    def outer(j, i, t_ref, s_ref):
        u = factor(j, i)
        s, t = s_ref[j, i], t_ref[j, i]
        s_around = beside(s) + (s_ref[j, i - 1] + s_ref[j, i + 1])
        t_around = beside(t) + (t_ref[j, i - 1] + t_ref[j, i + 1])
        halves = (4.0 / 3.0 * centre_half) * s + (4.0 / 3.0 * half) * s_around
        whole = (centre_full / 3.0) * t + (coupling_full / 3.0) * t_around
        return u * (halves - u * whole)

    p_one, t_one, s_one, p_two, t_two, s_two = scratch

    def start(i):
        for j in range(arms):
            enter(j, i, values(j, i), p_one, t_one)

    def between(i):
        for j in range(arms):
            value = outer(j, i, t_one, s_one)
            middle(j, i, value)
            enter(j, i, value, p_two, t_two)

    def finish(i):
        for j in range(arms):
            store(j, i, outer(j, i, t_two, s_two))

    first, last = block - 2 * reach, 3 * block + 2 * reach
    wavefront(
        [
            (first, last, start),
            (first + 1, last - 1, lambda i: inner(i, p_one, s_one)),
            (first + 2, last - 2, between),
            (first + 3, last - 3, lambda i: inner(i, p_two, s_two)),
            (first + 4, last - 4, finish),
        ]
    )


def pack_kernel(starts, fields, field_ref, other_ref, own_ref):
    arms = starts.shape[0] // 2
    side = lax.rem(lax.axis_index("space"), 2)
    field_ref[...] = fields[lax.rem(lax.axis_index("arm"), 2)]
    for j in range(arms):
        other_ref[j] = starts[(1 - side) * arms + j]
        own_ref[j] = starts[side * arms + j]


def places(block):
    side = lax.rem(lax.axis_index("space"), 2)
    return block + side * block, 2 * block - side * block, 3 * block * (1 - side), 3 * block * side


def window_kernel(starts, across, out_ref):
    arms = across.shape[0]
    side = lax.rem(lax.axis_index("space"), 2)
    for j in range(arms):
        out_ref[j] = starts[side * arms + j]
        out_ref[arms + j] = across[j]


def forward_kernel(
    labels, window, swap, straight, fields, f_swap, g_swap, piece, piece_core, piece_chip, piece_both,
    u_ref, one_ref, low_ref, high_ref, keep_ref, send_ref,
    q_ref, product_ref, *scratch,
):
    block = fields.shape[1]
    arms = swap.shape[0]
    side = lax.rem(lax.axis_index("space"), 2)
    core = lax.rem(lax.axis_index("arm"), 2)
    own_at, swap_at, straight_at, across_at = places(block)
    chip = lax.div(lax.axis_index("arm"), 2)
    here_at = straight_at + chip * (across_at - straight_at)
    there_at = across_at + chip * (straight_at - across_at)

    def gain(field):
        return jnp.exp(field * (-contour_step / 4))

    def fill(i, _):
        for kind in range(2):
            u_ref[kind, own_at + i] = gain(fields[kind, i])
        u_ref[core, here_at + i] = gain(piece[i])
        u_ref[1 - core, here_at + i] = gain(piece_core[i])
        u_ref[core, there_at + i] = gain(piece_chip[i])
        u_ref[1 - core, there_at + i] = gain(piece_both[i])
        u_ref[core, swap_at + i] = gain(f_swap[i])
        u_ref[1 - core, swap_at + i] = gain(g_swap[i])
        for j in range(arms):
            q_ref[j, own_at + i] = window[j, i]
            q_ref[j, across_at + i] = window[arms + j, i]
            q_ref[j, swap_at + i] = swap[j, i]
            q_ref[j, straight_at + i] = straight[j, i]

    lax.fori_loop(0, block, fill, None)
    kinds = [labels[side * arms + j] for j in range(arms)]

    def factor(j, i):
        return u_ref[kinds[j], i]

    def values(j, i):
        return q_ref[j, i]

    def store(j, i, value):
        q_ref[j, i] = value

    def middle(j, i, value):
        middle_ref[j, i] = value

    *scratch, middle_ref = scratch
    two_steps(block, arms, factor, values, middle, store, scratch)
    for j in range(arms):
        one_ref[j] = middle_ref[j, block : 3 * block]

    def finish(i, _):
        low, high = q_ref[0, block + i], q_ref[0, 2 * block + i]
        low_ref[0, i], high_ref[0, i] = low, high
        for j in range(1, arms):
            low_next, high_next = q_ref[j, block + i], q_ref[j, 2 * block + i]
            low_ref[j, i], high_ref[j, i] = low_next, high_next
            low, high = low * low_next, high * high_next
        product_ref[0, i], product_ref[1, i] = low, high
        keep_ref[i] = product_ref[core, i]
        send_ref[i] = product_ref[1 - core, i]

    lax.fori_loop(0, block, finish, None)


def backward_kernel(
    labels, u_ref, one_ref, two_left, two_low, two_high, two_right,
    j_mine, j_other, j_halo, j_halo_other,
    keep_ref, send_ref,
    junction_ref, q_ref, density_ref, middle_ref, *scratch,
):
    arms, block = two_low.shape[0], two_low.shape[1]
    side = lax.rem(lax.axis_index("space"), 2)
    core = lax.rem(lax.axis_index("arm"), 2)
    kinds = [labels[side * arms + j] for j in range(arms)]

    def fill(i, _):
        junction_ref[block + core * block + i] = j_mine[i]
        junction_ref[2 * block - core * block + i] = j_other[i]
        junction_ref[3 * block * (1 - core) + i] = j_halo[i]
        junction_ref[3 * block * core + i] = j_halo_other[i]
        for place, two in enumerate((two_left, two_low, two_high, two_right)):
            whole = junction_ref[place * block + i]
            for j in range(arms):
                q_ref[j, place * block + i] = whole / two[j, i]

    lax.fori_loop(0, block, fill, None)

    def factor(j, i):
        return u_ref[kinds[j], i]

    def values(j, i):
        return q_ref[j, i]

    def store(j, i, value):
        q_ref[j, i] = value

    def middle(j, i, value):
        middle_ref[j, i] = value

    two_steps(block, arms, factor, values, middle, store, scratch)

    is_a = [(kind == 0).astype(jnp.float32) for kind in kinds]

    def segment(i, _):
        quarter = 0.25 * junction_ref[block + i]
        total_a = total_b = None
        for j in range(arms):
            value = 0.5 * one_ref[j, i] * middle_ref[j, block + i] + 0.25 * q_ref[j, block + i] + quarter
            part_a, part_b = is_a[j] * value, (1.0 - is_a[j]) * value
            total_a = part_a if j == 0 else total_a + part_a
            total_b = part_b if j == 0 else total_b + part_b
        density_ref[0, i], density_ref[1, i] = total_a, total_b

    lax.fori_loop(0, 2 * block, segment, None)
    chips, owned = keep_ref.shape[0], keep_ref.shape[4]

    def spread(i, _):
        for chip in range(chips):
            mine = pl.ds(pl.multiple_of((2 * chip + core) * owned, 8), owned)
            other = pl.ds(pl.multiple_of((2 * chip + 1 - core) * owned, 8), owned)
            for part in range(2):
                for kind in range(2):
                    keep_ref[chip, part, kind, i] = density_ref[kind, part * block + i, mine]
                    send_ref[chip, part, kind, i] = density_ref[kind, part * block + i, other]

    lax.fori_loop(0, block, spread, None)


def total_kernel(*refs):
    *blocks, total_ref = refs
    total = jnp.zeros_like(total_ref)
    for block in blocks:
        for i in range(block.shape[0]):
            total = total + jnp.sum(block[i].reshape(-1, *total_ref.shape), axis=0)
    total_ref[...] = total


def meet_kernel(keep, received, own_ref, *out_refs):
    chips = keep.shape[0]
    side = lax.rem(lax.axis_index("space"), 2)
    chip = lax.div(lax.axis_index("arm"), 2)
    own_ref[...] = keep[chip, side] + received[chip, side]
    for out_ref, (step, flip) in zip(out_refs, other_chips(chips)):
        to_chip = lax.rem(chip + step, chips)
        to_side = 1 - side if flip else side
        out_ref[...] = keep[to_chip, to_side] + received[to_chip, to_side]


def final_kernel(cell_count, arm_count, fields, total, own, *refs):
    *others, density_ref, new_ref = refs
    owned = own.shape[2]
    scale = cell_count / (arm_count * jnp.sum(total[...]))
    rows = pl.ds(pl.multiple_of(lax.axis_index("arm") * owned, 8), owned)
    density = own[...]
    for other in others:
        density = density + other[...]
    density = density * scale
    density_ref[...] = density
    field_a, field_b = fields[0, :, rows], fields[1, :, rows]
    pressure = 0.5 * (field_a + field_b - chi_value)
    new_ref[0] = field_a + mixing * (chi_value * density[1] + pressure - field_a)
    new_ref[1] = field_b + mixing * (chi_value * density[0] + pressure - field_b)


def other_chips(chips):
    return [(step, flip) for step in range(chips) for flip in (False, True) if step or flip]


def vmem(shape):
    return pltpu.VMEM(shape, jnp.float32)


def f32(shape):
    return jax.ShapeDtypeStruct(shape, jnp.float32)


def call(kernel, out_shape, scratch, smem, *args, cost=1_000_000):
    specs = [pl.BlockSpec(memory_space=pltpu.SMEM if k < smem else pltpu.VMEM) for k in range(len(args))]
    return pl.pallas_call(
        kernel,
        out_shape=out_shape,
        in_specs=specs,
        out_specs=jax.tree.map(lambda _: pl.BlockSpec(memory_space=pltpu.VMEM), out_shape),
        scratch_shapes=scratch,
        compiler_params=pltpu.CompilerParams(vmem_limit_bytes=40 * 1024 * 1024),
        cost_estimate=pl.CostEstimate(flops=cost, bytes_accessed=cost, transcendentals=0),
    )(*args)


def local(fields, starts, labels):
    arm_size, space_size = lax.axis_size("arm"), lax.axis_size("space")
    chips, pairs = arm_size // 2, space_size // 2
    held, block, rows, columns = starts.shape
    arms = held // 2
    owned = rows // arm_size
    if chips != 2 or held % 2 or space_size % 2:
        raise ValueError("unsupported mesh")
    side = lax.rem(lax.axis_index("space"), 2)
    core = lax.rem(lax.axis_index("arm"), 2)

    def send(value, target):
        perm = []
        for a in range(arm_size):
            for s in range(space_size):
                chip_to, core_to, pair_to, side_to = target(a // 2, a % 2, s // 2, s % 2)
                to = (2 * (chip_to % chips) + core_to) * space_size + 2 * (pair_to % pairs) + side_to
                perm.append((a * space_size + s, to))
        return lax.ppermute(value, AXES, perm)

    def to_core(value):
        return send(value, lambda x, c, p, h: (x, 1 - c, p, h))

    def to_side(value):
        return send(value, lambda x, c, p, h: (x, c, p, 1 - h))

    def to_straight(value):
        return send(value, lambda x, c, p, h: (x, c, p + 2 * h - 1, h))

    def to_across(value):
        return send(value, lambda x, c, p, h: (x, c, p + 2 * h - 1, 1 - h))

    field_own, other_set, own_set = call(
        pack_kernel,
        (
            f32((block, rows, columns)),
            f32((arms, block, rows, columns)),
            f32((arms, block, rows, columns)),
        ),
        [],
        0,
        starts,
        fields,
    )
    field_got = send(field_own, lambda x, c, p, h: (x, c, p + 2 * h - 1, 1 - h if x else h))
    across = to_across(other_set)
    swap = to_side(other_set)
    straight = to_straight(own_set)
    pieces = [
        field_got,
        to_core(field_got),
        send(field_got, lambda x, c, p, h: (1 - x, c, p, h)),
        send(field_got, lambda x, c, p, h: (1 - x, 1 - c, p, h)),
    ]
    field_swap = to_side(field_own)
    swap_more = to_core(field_swap)

    wide = vmem((arms, 4 * block, rows, columns))
    whole = (arms, 2 * block, rows, columns)
    part = (arms, block, rows, columns)
    one = (block, rows, columns)
    window = call(window_kernel, f32((2 * arms, block, rows, columns)), [], 0, starts, across)
    factor, step_one, low, high, keep, give = call(
        forward_kernel,
        (f32((2, 4 * block, rows, columns)), f32(whole), f32(part), f32(part), f32(one), f32(one)),
        [wide, vmem((2,) + one)] + [wide] * 7,
        1,
        labels, window, swap, straight, fields, field_swap, swap_more, *pieces,
        cost=8_000_000,
    )
    right = send(low, lambda x, c, p, h: (x, c, p - 1, h))
    left = send(high, lambda x, c, p, h: (x, c, p + 1, h))
    mine = keep * to_core(give)
    mine = mine * to_side(mine)
    junction = mine
    for step in range(1, chips):
        junction = junction * send(mine, lambda x, c, p, h, step=step: (x + step, c, p, h))
    halo = send(junction, lambda x, c, p, h: (x, c, p + 2 * c - 1, h))
    held_junction, left, right = lax.optimization_barrier((junction, left, right))
    junction_other = to_core(held_junction)
    halo_other = to_core(halo)

    total = call(total_kernel, f32((8, columns)), [], 0, junction, junction_other, halo, halo_other, cost=1)
    if pairs & (pairs - 1) == 0:
        step = 2
        while step < pairs:
            total = total + send(total, lambda x, c, p, h, step=step: (x, c, p + step, h))
            step *= 2
    else:
        total = lax.psum(total, "space") / 4.0
    parts = (chips, 2, 2, block, owned, columns)
    keep, give = call(
        backward_kernel,
        (f32(parts), f32(parts)),
        [vmem((4 * block, rows, columns)), wide, vmem((2,) + whole[1:])] + [wide] * 7,
        1,
        labels, factor, step_one, left, low, high, right, junction, junction_other, halo, halo_other,
        cost=8_000_000,
    )
    to_places = other_chips(chips)
    own, *gives = call(
        meet_kernel, (f32(parts[2:]),) * (1 + len(to_places)), [], 0, keep, to_core(give)
    )
    received = [
        send(value, lambda x, c, p, h, step=step, flip=flip: (x + step, c, p, 1 - h if flip else h))
        for value, (step, flip) in zip(gives, to_places)
    ]
    cell_count = block * space_size * rows * columns
    return call(
        functools.partial(final_kernel, cell_count, held * arm_size),
        (f32(parts[2:]), f32(parts[2:])),
        [],
        0,
        fields, total, own, *received,
    )


def solution(mesh):
    in_specs = (P(None, "space", None, None), P("arm", "space", None, None), P("arm"))
    out_specs = (P(None, "space", "arm", None), P(None, "space", "arm", None))
    return jax.shard_map(local, mesh=mesh, in_specs=in_specs, out_specs=out_specs, check_vma=False)
```

```python
import functools

import jax
import jax.numpy as jnp
from jax import lax
from jax.experimental import pallas as pl
from jax.experimental.pallas import tpu as pltpu
from jax.sharding import PartitionSpec as P

coupling_full = 0.15
contour_step = 0.05
chi_value = 2.0
mixing = 0.5
reach = 2

AXES = ("arm", "space")


def beside(plane):
    rows, columns = plane.shape
    total = pltpu.roll(plane, 1, 0) + pltpu.roll(plane, rows - 1, 0)
    return total + (pltpu.roll(plane, 1, 1) + pltpu.roll(plane, columns - 1, 1))


def wavefront(stages):
    runs = [(first + 2 * k, last + 2 * k, 2 * k, work) for k, (first, last, work) in enumerate(stages)]
    cuts = sorted({edge for first, last, _, _ in runs for edge in (first, last)})
    for begin, end in zip(cuts, cuts[1:]):
        active = [(lag, work) for first, last, lag, work in runs if first <= begin and end <= last]

        def body(i, _, active=active):
            for lag, work in reversed(active):
                work(i - lag)

        lax.fori_loop(begin, end, body, None)


def two_steps(block, arms, factor, values, middle, store, scratch):
    half = coupling_full / 2
    centre_half, centre_full = 1.0 - 6.0 * half, 1.0 - 6.0 * coupling_full

    def enter(j, i, value, p_ref, t_ref):
        u = factor(j, i)
        p = u * value
        p_ref[j, i] = p
        t_ref[j, i] = u * p

    def inner(i, p_ref, s_ref):
        for j in range(arms):
            u = factor(j, i)
            p = p_ref[j, i]
            around = beside(p) + (p_ref[j, i - 1] + p_ref[j, i + 1])
            s_ref[j, i] = (u * u) * (centre_half * p + half * around)

    def outer(j, i, t_ref, s_ref):
        u = factor(j, i)
        s, t = s_ref[j, i], t_ref[j, i]
        s_around = beside(s) + (s_ref[j, i - 1] + s_ref[j, i + 1])
        t_around = beside(t) + (t_ref[j, i - 1] + t_ref[j, i + 1])
        halves = (4.0 / 3.0 * centre_half) * s + (4.0 / 3.0 * half) * s_around
        whole = (centre_full / 3.0) * t + (coupling_full / 3.0) * t_around
        return u * (halves - u * whole)

    p_one, t_one, s_one, p_two, t_two, s_two = scratch

    def start(i):
        for j in range(arms):
            enter(j, i, values(j, i), p_one, t_one)

    def between(i):
        for j in range(arms):
            value = outer(j, i, t_one, s_one)
            middle(j, i, value)
            enter(j, i, value, p_two, t_two)

    def finish(i):
        for j in range(arms):
            store(j, i, outer(j, i, t_two, s_two))

    first, last = block - 2 * reach, 3 * block + 2 * reach
    wavefront(
        [
            (first, last, start),
            (first + 1, last - 1, lambda i: inner(i, p_one, s_one)),
            (first + 2, last - 2, between),
            (first + 3, last - 3, lambda i: inner(i, p_two, s_two)),
            (first + 4, last - 4, finish),
        ]
    )


def pack_kernel(starts, fields, field_ref, other_ref, own_ref):
    arms = starts.shape[0] // 2
    side = lax.rem(lax.axis_index("space"), 2)
    field_ref[...] = fields[lax.rem(lax.axis_index("arm"), 2)]
    for j in range(arms):
        other_ref[j] = starts[(1 - side) * arms + j]
        own_ref[j] = starts[side * arms + j]


def places(block):
    side = lax.rem(lax.axis_index("space"), 2)
    return block + side * block, 2 * block - side * block, 3 * block * (1 - side), 3 * block * side


def window_kernel(starts, across, out_ref):
    arms = across.shape[0]
    side = lax.rem(lax.axis_index("space"), 2)
    for j in range(arms):
        out_ref[j] = starts[side * arms + j]
        out_ref[arms + j] = across[j]


def forward_kernel(
    labels, window, swap, straight, fields, f_swap, g_swap, piece, piece_core, piece_chip, piece_both,
    u_ref, one_ref, low_ref, high_ref, keep_ref, send_ref,
    q_ref, product_ref, *scratch,
):
    block = fields.shape[1]
    arms = swap.shape[0]
    side = lax.rem(lax.axis_index("space"), 2)
    core = lax.rem(lax.axis_index("arm"), 2)
    own_at, swap_at, straight_at, across_at = places(block)
    chip = lax.div(lax.axis_index("arm"), 2)
    here_at = straight_at + chip * (across_at - straight_at)
    there_at = across_at + chip * (straight_at - across_at)

    def gain(field):
        return jnp.exp(field * (-contour_step / 4))

    def fill(i, _):
        for kind in range(2):
            u_ref[kind, own_at + i] = gain(fields[kind, i])
        u_ref[core, here_at + i] = gain(piece[i])
        u_ref[1 - core, here_at + i] = gain(piece_core[i])
        u_ref[core, there_at + i] = gain(piece_chip[i])
        u_ref[1 - core, there_at + i] = gain(piece_both[i])
        u_ref[core, swap_at + i] = gain(f_swap[i])
        u_ref[1 - core, swap_at + i] = gain(g_swap[i])
        for j in range(arms):
            q_ref[j, own_at + i] = window[j, i]
            q_ref[j, across_at + i] = window[arms + j, i]
            q_ref[j, swap_at + i] = swap[j, i]
            q_ref[j, straight_at + i] = straight[j, i]

    lax.fori_loop(0, block, fill, None)
    kinds = [labels[side * arms + j] for j in range(arms)]

    def factor(j, i):
        return u_ref[kinds[j], i]

    def values(j, i):
        return q_ref[j, i]

    def store(j, i, value):
        q_ref[j, i] = value

    def middle(j, i, value):
        middle_ref[j, i] = value

    *scratch, middle_ref = scratch
    two_steps(block, arms, factor, values, middle, store, scratch)
    for j in range(arms):
        one_ref[j] = middle_ref[j, block : 3 * block]

    def finish(i, _):
        low, high = q_ref[0, block + i], q_ref[0, 2 * block + i]
        low_ref[0, i], high_ref[0, i] = low, high
        for j in range(1, arms):
            low_next, high_next = q_ref[j, block + i], q_ref[j, 2 * block + i]
            low_ref[j, i], high_ref[j, i] = low_next, high_next
            low, high = low * low_next, high * high_next
        product_ref[0, i], product_ref[1, i] = low, high
        keep_ref[i] = product_ref[core, i]
        send_ref[i] = product_ref[1 - core, i]

    lax.fori_loop(0, block, finish, None)


def backward_kernel(
    labels, u_ref, one_ref, two_left, two_low, two_high, two_right,
    j_mine, j_other, j_halo, j_halo_other,
    keep_ref, send_ref,
    junction_ref, q_ref, density_ref, middle_ref, *scratch,
):
    arms, block = two_low.shape[0], two_low.shape[1]
    side = lax.rem(lax.axis_index("space"), 2)
    core = lax.rem(lax.axis_index("arm"), 2)
    kinds = [labels[side * arms + j] for j in range(arms)]

    def fill(i, _):
        junction_ref[block + core * block + i] = j_mine[i]
        junction_ref[2 * block - core * block + i] = j_other[i]
        junction_ref[3 * block * (1 - core) + i] = j_halo[i]
        junction_ref[3 * block * core + i] = j_halo_other[i]
        for place, two in enumerate((two_left, two_low, two_high, two_right)):
            whole = junction_ref[place * block + i]
            for j in range(arms):
                q_ref[j, place * block + i] = whole / two[j, i]

    lax.fori_loop(0, block, fill, None)

    def factor(j, i):
        return u_ref[kinds[j], i]

    def values(j, i):
        return q_ref[j, i]

    def store(j, i, value):
        q_ref[j, i] = value

    def middle(j, i, value):
        middle_ref[j, i] = value

    two_steps(block, arms, factor, values, middle, store, scratch)

    is_a = [(kind == 0).astype(jnp.float32) for kind in kinds]

    def segment(i, _):
        quarter = 0.25 * junction_ref[block + i]
        total_a = total_b = None
        for j in range(arms):
            value = 0.5 * one_ref[j, i] * middle_ref[j, block + i] + 0.25 * q_ref[j, block + i] + quarter
            part_a, part_b = is_a[j] * value, (1.0 - is_a[j]) * value
            total_a = part_a if j == 0 else total_a + part_a
            total_b = part_b if j == 0 else total_b + part_b
        density_ref[0, i], density_ref[1, i] = total_a, total_b

    lax.fori_loop(0, 2 * block, segment, None)
    chips, owned = keep_ref.shape[0], keep_ref.shape[4]

    def spread(i, _):
        for chip in range(chips):
            mine = pl.ds(pl.multiple_of((2 * chip + core) * owned, 8), owned)
            other = pl.ds(pl.multiple_of((2 * chip + 1 - core) * owned, 8), owned)
            for part in range(2):
                for kind in range(2):
                    keep_ref[chip, part, kind, i] = density_ref[kind, part * block + i, mine]
                    send_ref[chip, part, kind, i] = density_ref[kind, part * block + i, other]

    lax.fori_loop(0, block, spread, None)


def product_kernel(one, other, *out_refs):
    planes = one.shape[0] // len(out_refs)
    for k, out_ref in enumerate(out_refs):
        part = slice(k * planes, (k + 1) * planes)
        out_ref[...] = one[part] * other[part]


def join_kernel(upper, upper_other, lower, lower_other, out_ref):
    planes = upper.shape[0]
    out_ref[:planes] = upper[...] * upper_other[...]
    out_ref[planes:] = lower[...] * lower_other[...]


def total_kernel(*refs):
    *blocks, total_ref = refs
    total = jnp.zeros_like(total_ref)
    for block in blocks:
        for i in range(block.shape[0]):
            total = total + jnp.sum(block[i].reshape(-1, *total_ref.shape), axis=0)
    total_ref[...] = total


def meet_kernel(keep, received, own_ref, *out_refs):
    chips = keep.shape[0]
    side = lax.rem(lax.axis_index("space"), 2)
    chip = lax.div(lax.axis_index("arm"), 2)
    own_ref[...] = keep[chip, side] + received[chip, side]
    for out_ref, (step, flip) in zip(out_refs, other_chips(chips)):
        to_chip = lax.rem(chip + step, chips)
        to_side = 1 - side if flip else side
        out_ref[...] = keep[to_chip, to_side] + received[to_chip, to_side]


def final_kernel(cell_count, arm_count, fields, total, own, *refs):
    *others, density_ref, new_ref = refs
    owned = own.shape[2]
    scale = cell_count / (arm_count * jnp.sum(total[...]))
    rows = pl.ds(pl.multiple_of(lax.axis_index("arm") * owned, 8), owned)
    density = own[...]
    for other in others:
        density = density + other[...]
    density = density * scale
    density_ref[...] = density
    field_a, field_b = fields[0, :, rows], fields[1, :, rows]
    pressure = 0.5 * (field_a + field_b - chi_value)
    new_ref[0] = field_a + mixing * (chi_value * density[1] + pressure - field_a)
    new_ref[1] = field_b + mixing * (chi_value * density[0] + pressure - field_b)


def other_chips(chips):
    return [(step, flip) for step in range(chips) for flip in (False, True) if step or flip]


def vmem(shape):
    return pltpu.VMEM(shape, jnp.float32)


def f32(shape):
    return jax.ShapeDtypeStruct(shape, jnp.float32)


def call(kernel, out_shape, scratch, smem, *args, cost=1_000_000):
    specs = [pl.BlockSpec(memory_space=pltpu.SMEM if k < smem else pltpu.VMEM) for k in range(len(args))]
    return pl.pallas_call(
        kernel,
        out_shape=out_shape,
        in_specs=specs,
        out_specs=jax.tree.map(lambda _: pl.BlockSpec(memory_space=pltpu.VMEM), out_shape),
        scratch_shapes=scratch,
        compiler_params=pltpu.CompilerParams(vmem_limit_bytes=40 * 1024 * 1024),
        cost_estimate=pl.CostEstimate(flops=cost, bytes_accessed=cost, transcendentals=0),
    )(*args)


def local(fields, starts, labels):
    arm_size, space_size = lax.axis_size("arm"), lax.axis_size("space")
    chips, pairs = arm_size // 2, space_size // 2
    held, block, rows, columns = starts.shape
    arms = held // 2
    owned = rows // arm_size
    if chips != 2 or held % 2 or space_size % 2 or block % 2:
        raise ValueError("unsupported mesh")
    side = lax.rem(lax.axis_index("space"), 2)
    core = lax.rem(lax.axis_index("arm"), 2)

    def send(value, target):
        perm = []
        for a in range(arm_size):
            for s in range(space_size):
                chip_to, core_to, pair_to, side_to = target(a // 2, a % 2, s // 2, s % 2)
                to = (2 * (chip_to % chips) + core_to) * space_size + 2 * (pair_to % pairs) + side_to
                perm.append((a * space_size + s, to))
        return lax.ppermute(value, AXES, perm)

    def to_core(value):
        return send(value, lambda x, c, p, h: (x, 1 - c, p, h))

    def to_side(value):
        return send(value, lambda x, c, p, h: (x, c, p, 1 - h))

    def to_chip(value):
        return send(value, lambda x, c, p, h: (x + 1, c, p, h))

    def to_straight(value):
        return send(value, lambda x, c, p, h: (x, c, p + 2 * h - 1, h))

    def to_across(value):
        return send(value, lambda x, c, p, h: (x, c, p + 2 * h - 1, 1 - h))

    field_own, other_set, own_set = call(
        pack_kernel,
        (
            f32((block, rows, columns)),
            f32((arms, block, rows, columns)),
            f32((arms, block, rows, columns)),
        ),
        [],
        0,
        starts,
        fields,
    )
    field_got = send(field_own, lambda x, c, p, h: (x, c, p + 2 * h - 1, 1 - h if x else h))
    across = to_across(other_set)
    swap = to_side(other_set)
    straight = to_straight(own_set)
    field_both = send(field_got, lambda x, c, p, h: (1 - x, 1 - c, p, h))
    pieces = [field_got, to_core(field_got), to_core(field_both), field_both]
    field_swap = to_side(field_own)
    swap_more = to_core(field_swap)

    wide = vmem((arms, 4 * block, rows, columns))
    whole = (arms, 2 * block, rows, columns)
    part = (arms, block, rows, columns)
    one = (block, rows, columns)
    window = call(window_kernel, f32((2 * arms, block, rows, columns)), [], 0, starts, across)
    factor, step_one, low, high, keep, give = call(
        forward_kernel,
        (f32((2, 4 * block, rows, columns)), f32(whole), f32(part), f32(part), f32(one), f32(one)),
        [wide, vmem((2,) + one)] + [wide] * 7,
        1,
        labels, window, swap, straight, fields, field_swap, swap_more, *pieces,
        cost=8_000_000,
    )
    right = send(low, lambda x, c, p, h: (x, c, p - 1, h))
    left = send(high, lambda x, c, p, h: (x, c, p + 1, h))
    half = f32((block // 2, rows, columns))
    upper, lower = call(product_kernel, (half, half), [], 0, keep, to_core(give))
    upper = call(product_kernel, (half,), [], 0, upper, to_side(upper))[0]
    lower = call(product_kernel, (half,), [], 0, lower, to_chip(lower))[0]
    junction = call(join_kernel, f32(one), [], 0, upper, to_chip(upper), lower, to_side(lower))
    halo = send(junction, lambda x, c, p, h: (x, c, p + 2 * c - 1, h))
    held_junction, left, right = lax.optimization_barrier((junction, left, right))
    junction_other = to_core(held_junction)
    halo_other = to_core(halo)

    total = call(total_kernel, f32((8, columns)), [], 0, junction, junction_other, halo, halo_other, cost=1)
    if pairs & (pairs - 1) == 0:
        step = 2
        while step < pairs:
            total = total + send(total, lambda x, c, p, h, step=step: (x, c, p + step, h))
            step *= 2
    else:
        total = lax.psum(total, "space") / 4.0
    parts = (chips, 2, 2, block, owned, columns)
    keep, give = call(
        backward_kernel,
        (f32(parts), f32(parts)),
        [vmem((4 * block, rows, columns)), wide, vmem((2,) + whole[1:])] + [wide] * 7,
        1,
        labels, factor, step_one, left, low, high, right, junction, junction_other, halo, halo_other,
        cost=8_000_000,
    )
    to_places = other_chips(chips)
    own, *gives = call(
        meet_kernel, (f32(parts[2:]),) * (1 + len(to_places)), [], 0, keep, to_core(give)
    )
    received = [
        send(value, lambda x, c, p, h, step=step, flip=flip: (x + step, c, p, 1 - h if flip else h))
        for value, (step, flip) in zip(gives, to_places)
    ]
    cell_count = block * space_size * rows * columns
    return call(
        functools.partial(final_kernel, cell_count, held * arm_size),
        (f32(parts[2:]), f32(parts[2:])),
        [],
        0,
        fields, total, own, *received,
    )


def solution(mesh):
    in_specs = (P(None, "space", None, None), P("arm", "space", None, None), P("arm"))
    out_specs = (P(None, "space", "arm", None), P(None, "space", "arm", None))
    return jax.shard_map(local, mesh=mesh, in_specs=in_specs, out_specs=out_specs, check_vma=False)
```

```python
import functools

import jax
import jax.numpy as jnp
from jax import lax
from jax.experimental import pallas as pl
from jax.experimental.pallas import tpu as pltpu
from jax.sharding import PartitionSpec as P

coupling_full = 0.15
contour_step = 0.05
chi_value = 2.0
mixing = 0.5
reach = 2

AXES = ("arm", "space")


def shifts(plane, axis):
    return pltpu.roll(plane, 1, axis), pltpu.roll(plane, plane.shape[axis] - 1, axis)


def wavefront(stages):
    runs = [(first + 2 * k, last + 2 * k, 2 * k, work) for k, (first, last, work) in enumerate(stages)]
    cuts = sorted({edge for first, last, _, _ in runs for edge in (first, last)})
    for begin, end in zip(cuts, cuts[1:]):
        active = [(lag, work) for first, last, lag, work in runs if first <= begin and end <= last]

        def body(i, _, active=active):
            for lag, work in reversed(active):
                work(i - lag)

        lax.fori_loop(begin, end, body, None)


def two_steps(block, arms, factor, factor_shifts, values, middle, store, scratch):
    half = coupling_full / 2
    centre_half, centre_full = 1.0 - 6.0 * half, 1.0 - 6.0 * coupling_full

    def enter(j, i, value, p_ref, t_ref):
        u = factor(j, i)
        p = u * value
        p_ref[j, i] = p
        t_ref[j, i] = u * p

    def inner(i, p_ref, s_ref, z_ref):
        for j in range(arms):
            u = factor(j, i)
            p = p_ref[j, i]
            (up, down), (left, right) = shifts(p, 0), shifts(p, 1)
            u_left, u_right = factor_shifts(j, i)
            z_ref[j, i] = u_left * left + u_right * right
            around = (up + down) + (left + right) + (p_ref[j, i - 1] + p_ref[j, i + 1])
            s_ref[j, i] = (u * u) * (centre_half * p + half * around)

    def outer(j, i, t_ref, s_ref, z_ref):
        u = factor(j, i)
        s, t = s_ref[j, i], t_ref[j, i]
        (up, down), (left, right) = shifts(s, 0), shifts(s, 1)
        s_around = (up + down) + (left + right) + (s_ref[j, i - 1] + s_ref[j, i + 1])
        up, down = shifts(t, 0)
        t_around = (up + down) + z_ref[j, i] + (t_ref[j, i - 1] + t_ref[j, i + 1])
        halves = (4.0 / 3.0 * centre_half) * s + (4.0 / 3.0 * half) * s_around
        whole = (centre_full / 3.0) * t + (coupling_full / 3.0) * t_around
        return u * (halves - u * whole)

    p_one, t_one, s_one, z_one, p_two, t_two, s_two, z_two = scratch

    def start(i):
        for j in range(arms):
            enter(j, i, values(j, i), p_one, t_one)

    def between(i):
        for j in range(arms):
            value = outer(j, i, t_one, s_one, z_one)
            middle(j, i, value)
            enter(j, i, value, p_two, t_two)

    def finish(i):
        for j in range(arms):
            store(j, i, outer(j, i, t_two, s_two, z_two))

    first, last = block - 2 * reach, 3 * block + 2 * reach
    wavefront(
        [
            (first, last, start),
            (first + 1, last - 1, lambda i: inner(i, p_one, s_one, z_one)),
            (first + 2, last - 2, between),
            (first + 3, last - 3, lambda i: inner(i, p_two, s_two, z_two)),
            (first + 4, last - 4, finish),
        ]
    )


def pack_kernel(starts, fields, field_ref, other_ref, own_ref):
    arms = starts.shape[0] // 2
    side = lax.rem(lax.axis_index("space"), 2)
    field_ref[...] = fields[lax.rem(lax.axis_index("arm"), 2)]
    for j in range(arms):
        other_ref[j] = starts[(1 - side) * arms + j]
        own_ref[j] = starts[side * arms + j]


def places(block):
    side = lax.rem(lax.axis_index("space"), 2)
    return block + side * block, 2 * block - side * block, 3 * block * (1 - side), 3 * block * side


def window_kernel(labels, starts, across, out_ref):
    arms = across.shape[0]
    side = lax.rem(lax.axis_index("space"), 2)
    for j in range(arms):
        out_ref[j] = starts[side * arms + j]
        out_ref[arms + j] = across[j]


def gain_kernel(
    fields, f_swap, g_swap, piece, piece_core, piece_chip, piece_both, u_ref, u_left_ref, u_right_ref
):
    block = fields.shape[1]
    core = lax.rem(lax.axis_index("arm"), 2)
    own_at, swap_at, straight_at, across_at = places(block)
    chip = lax.div(lax.axis_index("arm"), 2)
    here_at = straight_at + chip * (across_at - straight_at)
    there_at = across_at + chip * (straight_at - across_at)

    def gain(field):
        return jnp.exp(field * (-contour_step / 4))

    def fill(i, _):
        for kind in range(2):
            u_ref[kind, own_at + i] = gain(fields[kind, i])
        for at, mine, other in (
            (swap_at, f_swap, g_swap),
            (here_at, piece, piece_core),
            (there_at, piece_chip, piece_both),
        ):
            u_ref[core, at + i] = gain(mine[i])
            u_ref[1 - core, at + i] = gain(other[i])

    lax.fori_loop(0, block, fill, None)

    def shift(i, _):
        for kind in range(2):
            u_left_ref[kind, i], u_right_ref[kind, i] = shifts(u_ref[kind, i], 1)

    lax.fori_loop(0, 4 * block, shift, None, unroll=2)


def forward_kernel(
    labels, window, swap, straight, u_ref, u_left_ref, u_right_ref,
    one_ref, low_ref, high_ref, keep_ref, send_ref,
    q_ref, product_ref, *scratch,
):
    arms, block = swap.shape[0], swap.shape[1]
    side = lax.rem(lax.axis_index("space"), 2)
    core = lax.rem(lax.axis_index("arm"), 2)
    own_at, swap_at, straight_at, across_at = places(block)

    def fill(i, _):
        for j in range(arms):
            q_ref[j, own_at + i] = window[j, i]
            q_ref[j, across_at + i] = window[arms + j, i]
            q_ref[j, swap_at + i] = swap[j, i]
            q_ref[j, straight_at + i] = straight[j, i]

    lax.fori_loop(0, block, fill, None)
    kinds = [labels[side * arms + j] for j in range(arms)]

    def factor(j, i):
        return u_ref[kinds[j], i]

    def factor_shifts(j, i):
        return u_left_ref[kinds[j], i], u_right_ref[kinds[j], i]

    def values(j, i):
        return q_ref[j, i]

    def store(j, i, value):
        q_ref[j, i] = value

    def middle(j, i, value):
        middle_ref[j, i] = value

    *scratch, middle_ref = scratch
    two_steps(block, arms, factor, factor_shifts, values, middle, store, scratch)
    for j in range(arms):
        one_ref[j] = middle_ref[j, block : 3 * block]

    def finish(i, _):
        low, high = q_ref[0, block + i], q_ref[0, 2 * block + i]
        low_ref[0, i], high_ref[0, i] = low, high
        for j in range(1, arms):
            low_next, high_next = q_ref[j, block + i], q_ref[j, 2 * block + i]
            low_ref[j, i], high_ref[j, i] = low_next, high_next
            low, high = low * low_next, high * high_next
        product_ref[0, i], product_ref[1, i] = low, high
        keep_ref[i] = product_ref[core, i]
        send_ref[i] = product_ref[1 - core, i]

    lax.fori_loop(0, block, finish, None)


def backward_kernel(
    labels, u_ref, u_left_ref, u_right_ref, one_ref, two_left, two_low, two_high, two_right,
    j_mine, j_other, j_halo, j_halo_other,
    keep_ref, send_ref,
    junction_ref, q_ref, density_ref, middle_ref, *scratch,
):
    arms, block = two_low.shape[0], two_low.shape[1]
    side = lax.rem(lax.axis_index("space"), 2)
    core = lax.rem(lax.axis_index("arm"), 2)
    kinds = [labels[side * arms + j] for j in range(arms)]

    def fill(i, _):
        junction_ref[block + core * block + i] = j_mine[i]
        junction_ref[2 * block - core * block + i] = j_other[i]
        junction_ref[3 * block * (1 - core) + i] = j_halo[i]
        junction_ref[3 * block * core + i] = j_halo_other[i]
        for place, two in enumerate((two_left, two_low, two_high, two_right)):
            whole = junction_ref[place * block + i]
            for j in range(arms):
                q_ref[j, place * block + i] = whole / two[j, i]

    lax.fori_loop(0, block, fill, None)

    def factor(j, i):
        return u_ref[kinds[j], i]

    def factor_shifts(j, i):
        return u_left_ref[kinds[j], i], u_right_ref[kinds[j], i]

    def values(j, i):
        return q_ref[j, i]

    def store(j, i, value):
        q_ref[j, i] = value

    def middle(j, i, value):
        middle_ref[j, i] = value

    two_steps(block, arms, factor, factor_shifts, values, middle, store, scratch)

    is_a = [(kind == 0).astype(jnp.float32) for kind in kinds]

    def segment(i, _):
        quarter = 0.25 * junction_ref[block + i]
        total_a = total_b = None
        for j in range(arms):
            value = 0.5 * one_ref[j, i] * middle_ref[j, block + i] + 0.25 * q_ref[j, block + i] + quarter
            part_a, part_b = is_a[j] * value, (1.0 - is_a[j]) * value
            total_a = part_a if j == 0 else total_a + part_a
            total_b = part_b if j == 0 else total_b + part_b
        density_ref[0, i], density_ref[1, i] = total_a, total_b

    lax.fori_loop(0, 2 * block, segment, None)
    chips, owned = keep_ref.shape[0], keep_ref.shape[4]

    def spread(i, _):
        for chip in range(chips):
            mine = pl.ds(pl.multiple_of((2 * chip + core) * owned, 8), owned)
            other = pl.ds(pl.multiple_of((2 * chip + 1 - core) * owned, 8), owned)
            for part in range(2):
                for kind in range(2):
                    keep_ref[chip, part, kind, i] = density_ref[kind, part * block + i, mine]
                    send_ref[chip, part, kind, i] = density_ref[kind, part * block + i, other]

    lax.fori_loop(0, block, spread, None)


def product_kernel(one, other, *out_refs):
    planes = one.shape[0] // len(out_refs)
    for k, out_ref in enumerate(out_refs):
        part = slice(k * planes, (k + 1) * planes)
        out_ref[...] = one[part] * other[part]


def join_kernel(upper, upper_other, lower, lower_other, out_ref):
    planes = upper.shape[0]
    out_ref[:planes] = upper[...] * upper_other[...]
    out_ref[planes:] = lower[...] * lower_other[...]


def total_kernel(*refs):
    *blocks, total_ref = refs
    total = jnp.zeros_like(total_ref)
    for block in blocks:
        for i in range(block.shape[0]):
            total = total + jnp.sum(block[i].reshape(-1, *total_ref.shape), axis=0)
    total_ref[...] = total


def meet_kernel(keep, received, own_ref, *out_refs):
    chips = keep.shape[0]
    side = lax.rem(lax.axis_index("space"), 2)
    chip = lax.div(lax.axis_index("arm"), 2)
    own_ref[...] = keep[chip, side] + received[chip, side]
    for out_ref, (step, flip) in zip(out_refs, other_chips(chips)):
        to_chip = lax.rem(chip + step, chips)
        to_side = 1 - side if flip else side
        out_ref[...] = keep[to_chip, to_side] + received[to_chip, to_side]


def final_kernel(cell_count, arm_count, fields, total, own, *refs):
    *others, density_ref, new_ref = refs
    owned = own.shape[2]
    scale = cell_count / (arm_count * jnp.sum(total[...]))
    rows = pl.ds(pl.multiple_of(lax.axis_index("arm") * owned, 8), owned)
    density = own[...]
    for other in others:
        density = density + other[...]
    density = density * scale
    density_ref[...] = density
    field_a, field_b = fields[0, :, rows], fields[1, :, rows]
    pressure = 0.5 * (field_a + field_b - chi_value)
    new_ref[0] = field_a + mixing * (chi_value * density[1] + pressure - field_a)
    new_ref[1] = field_b + mixing * (chi_value * density[0] + pressure - field_b)


def other_chips(chips):
    return [(step, flip) for step in range(chips) for flip in (False, True) if step or flip]


def vmem(shape):
    return pltpu.VMEM(shape, jnp.float32)


def f32(shape):
    return jax.ShapeDtypeStruct(shape, jnp.float32)


def call(kernel, out_shape, scratch, smem, *args, cost=1_000_000):
    specs = [pl.BlockSpec(memory_space=pltpu.SMEM if k < smem else pltpu.VMEM) for k in range(len(args))]
    return pl.pallas_call(
        kernel,
        out_shape=out_shape,
        in_specs=specs,
        out_specs=jax.tree.map(lambda _: pl.BlockSpec(memory_space=pltpu.VMEM), out_shape),
        scratch_shapes=scratch,
        compiler_params=pltpu.CompilerParams(vmem_limit_bytes=40 * 1024 * 1024),
        cost_estimate=pl.CostEstimate(flops=cost, bytes_accessed=cost, transcendentals=0),
    )(*args)


def local(fields, starts, labels):
    arm_size, space_size = lax.axis_size("arm"), lax.axis_size("space")
    chips, pairs = arm_size // 2, space_size // 2
    held, block, rows, columns = starts.shape
    arms = held // 2
    owned = rows // arm_size
    if chips != 2 or held % 2 or space_size % 2 or block % 2:
        raise ValueError("unsupported mesh")
    side = lax.rem(lax.axis_index("space"), 2)
    core = lax.rem(lax.axis_index("arm"), 2)

    def send(value, target):
        perm = []
        for a in range(arm_size):
            for s in range(space_size):
                chip_to, core_to, pair_to, side_to = target(a // 2, a % 2, s // 2, s % 2)
                to = (2 * (chip_to % chips) + core_to) * space_size + 2 * (pair_to % pairs) + side_to
                perm.append((a * space_size + s, to))
        return lax.ppermute(value, AXES, perm)

    def to_core(value):
        return send(value, lambda x, c, p, h: (x, 1 - c, p, h))

    def to_side(value):
        return send(value, lambda x, c, p, h: (x, c, p, 1 - h))

    def to_chip(value):
        return send(value, lambda x, c, p, h: (x + 1, c, p, h))

    def to_straight(value):
        return send(value, lambda x, c, p, h: (x, c, p + 2 * h - 1, h))

    def to_across(value):
        return send(value, lambda x, c, p, h: (x, c, p + 2 * h - 1, 1 - h))

    field_own, other_set, own_set = call(
        pack_kernel,
        (
            f32((block, rows, columns)),
            f32((arms, block, rows, columns)),
            f32((arms, block, rows, columns)),
        ),
        [],
        0,
        starts,
        fields,
    )
    field_got = send(field_own, lambda x, c, p, h: (x, c, p + 2 * h - 1, 1 - h if x else h))
    across = to_across(other_set)
    swap = to_side(other_set)
    straight = to_straight(own_set)
    field_both = send(field_got, lambda x, c, p, h: (1 - x, 1 - c, p, h))
    pieces = [field_got, to_core(field_got), to_core(field_both), field_both]
    field_swap = to_side(field_own)
    swap_more = to_core(field_swap)

    wide = vmem((arms, 4 * block, rows, columns))
    whole = (arms, 2 * block, rows, columns)
    part = (arms, block, rows, columns)
    one = (block, rows, columns)
    window = call(window_kernel, f32((2 * arms, block, rows, columns)), [], 1, labels, starts, across)
    gains = f32((2, 4 * block, rows, columns))
    factors = call(gain_kernel, (gains,) * 3, [], 0, fields, field_swap, swap_more, *pieces)
    step_one, low, high, keep, give = call(
        forward_kernel,
        (f32(whole), f32(part), f32(part), f32(one), f32(one)),
        [wide, vmem((2,) + one)] + [wide] * 9,
        1,
        labels, window, swap, straight, *factors,
        cost=8_000_000,
    )
    right = send(low, lambda x, c, p, h: (x, c, p - 1, h))
    left = send(high, lambda x, c, p, h: (x, c, p + 1, h))
    half = f32((block // 2, rows, columns))
    upper, lower = call(product_kernel, (half, half), [], 0, keep, to_core(give))
    upper = call(product_kernel, (half,), [], 0, upper, to_side(upper))[0]
    lower = call(product_kernel, (half,), [], 0, lower, to_chip(lower))[0]
    junction = call(join_kernel, f32(one), [], 0, upper, to_chip(upper), lower, to_side(lower))
    halo = send(junction, lambda x, c, p, h: (x, c, p + 2 * c - 1, h))
    held_junction, left, right = lax.optimization_barrier((junction, left, right))
    junction_other = to_core(held_junction)
    halo_other = to_core(halo)

    total = call(total_kernel, f32((8, columns)), [], 0, junction, junction_other, halo, halo_other, cost=1)
    if pairs & (pairs - 1) == 0:
        step = 2
        while step < pairs:
            total = total + send(total, lambda x, c, p, h, step=step: (x, c, p + step, h))
            step *= 2
    else:
        total = lax.psum(total, "space") / 4.0
    parts = (chips, 2, 2, block, owned, columns)
    keep, give = call(
        backward_kernel,
        (f32(parts), f32(parts)),
        [vmem((4 * block, rows, columns)), wide, vmem((2,) + whole[1:])] + [wide] * 9,
        1,
        labels, *factors, step_one, left, low, high, right, junction, junction_other, halo, halo_other,
        cost=8_000_000,
    )
    to_places = other_chips(chips)
    own, *gives = call(
        meet_kernel, (f32(parts[2:]),) * (1 + len(to_places)), [], 0, keep, to_core(give)
    )
    received = [
        send(value, lambda x, c, p, h, step=step, flip=flip: (x + step, c, p, 1 - h if flip else h))
        for value, (step, flip) in zip(gives, to_places)
    ]
    cell_count = block * space_size * rows * columns
    return call(
        functools.partial(final_kernel, cell_count, held * arm_size),
        (f32(parts[2:]), f32(parts[2:])),
        [],
        0,
        fields, total, own, *received,
    )


def solution(mesh):
    in_specs = (P(None, "space", None, None), P("arm", "space", None, None), P("arm"))
    out_specs = (P(None, "space", "arm", None), P(None, "space", "arm", None))
    return jax.shard_map(local, mesh=mesh, in_specs=in_specs, out_specs=out_specs, check_vma=False)
```

```python
import functools

import jax
import jax.numpy as jnp
from jax import lax
from jax.experimental import pallas as pl
from jax.experimental.pallas import tpu as pltpu
from jax.sharding import PartitionSpec as P

coupling_full = 0.15
contour_step = 0.05
chi_value = 2.0
mixing = 0.5
reach = 2

AXES = ("arm", "space")


def shifts(plane, axis):
    return pltpu.roll(plane, 1, axis), pltpu.roll(plane, plane.shape[axis] - 1, axis)


def wavefront(stages):
    runs = [(first + 2 * k, last + 2 * k, 2 * k, work) for k, (first, last, work) in enumerate(stages)]
    cuts = sorted({edge for first, last, _, _ in runs for edge in (first, last)})
    for begin, end in zip(cuts, cuts[1:]):
        active = [(lag, work) for first, last, lag, work in runs if first <= begin and end <= last]

        def body(i, _, active=active):
            for lag, work in reversed(active):
                work(i - lag)

        lax.fori_loop(begin, end, body, None)


def two_steps(block, arms, factor, factor_shifts, values, middle, store, scratch):
    half = coupling_full / 2
    centre_half, centre_full = 1.0 - 6.0 * half, 1.0 - 6.0 * coupling_full

    def enter(j, i, value, p_ref, t_ref):
        u = factor(j, i)
        p = u * value
        p_ref[j, i] = p
        t_ref[j, i] = u * p

    def inner(i, p_ref, s_ref, z_ref):
        for j in range(arms):
            u = factor(j, i)
            p = p_ref[j, i]
            (up, down), (left, right) = shifts(p, 0), shifts(p, 1)
            u_left, u_right = factor_shifts(j, i)
            z_ref[j, i] = u_left * left + u_right * right
            around = (up + down) + (left + right) + (p_ref[j, i - 1] + p_ref[j, i + 1])
            s_ref[j, i] = (u * u) * (centre_half * p + half * around)

    def outer(j, i, t_ref, s_ref, z_ref):
        u = factor(j, i)
        s, t = s_ref[j, i], t_ref[j, i]
        (up, down), (left, right) = shifts(s, 0), shifts(s, 1)
        s_around = (up + down) + (left + right) + (s_ref[j, i - 1] + s_ref[j, i + 1])
        up, down = shifts(t, 0)
        t_around = (up + down) + z_ref[j, i] + (t_ref[j, i - 1] + t_ref[j, i + 1])
        halves = (4.0 / 3.0 * centre_half) * s + (4.0 / 3.0 * half) * s_around
        whole = (centre_full / 3.0) * t + (coupling_full / 3.0) * t_around
        return u * (halves - u * whole)

    p_one, t_one, s_one, z_one, p_two, t_two, s_two, z_two = scratch

    def start(i):
        for j in range(arms):
            enter(j, i, values(j, i), p_one, t_one)

    def between(i):
        for j in range(arms):
            value = outer(j, i, t_one, s_one, z_one)
            middle(j, i, value)
            enter(j, i, value, p_two, t_two)

    def finish(i):
        for j in range(arms):
            store(j, i, outer(j, i, t_two, s_two, z_two))

    first, last = block - 2 * reach, 3 * block + 2 * reach
    wavefront(
        [
            (first, last, start),
            (first + 1, last - 1, lambda i: inner(i, p_one, s_one, z_one)),
            (first + 2, last - 2, between),
            (first + 3, last - 3, lambda i: inner(i, p_two, s_two, z_two)),
            (first + 4, last - 4, finish),
        ]
    )


def pack_kernel(starts, other_ref, own_ref):
    arms = starts.shape[0] // 2
    side = lax.rem(lax.axis_index("space"), 2)
    for j in range(arms):
        other_ref[j] = starts[(1 - side) * arms + j]
        own_ref[j] = starts[side * arms + j]


def pick_kernel(fields, field_ref):
    field_ref[...] = fields[lax.rem(lax.axis_index("arm"), 2)]


def places(block):
    side = lax.rem(lax.axis_index("space"), 2)
    return block + side * block, 2 * block - side * block, 3 * block * (1 - side), 3 * block * side


def window_kernel(labels, starts, across, out_ref):
    arms = across.shape[0]
    side = lax.rem(lax.axis_index("space"), 2)
    for j in range(arms):
        out_ref[j] = starts[side * arms + j]
        out_ref[arms + j] = across[j]


def gain_kernel(
    fields, f_swap, g_swap, piece, piece_core, piece_chip, piece_both, u_ref, u_left_ref, u_right_ref
):
    block = fields.shape[1]
    core = lax.rem(lax.axis_index("arm"), 2)
    own_at, swap_at, straight_at, across_at = places(block)
    chip = lax.div(lax.axis_index("arm"), 2)
    here_at = straight_at + chip * (across_at - straight_at)
    there_at = across_at + chip * (straight_at - across_at)

    def gain(field):
        return jnp.exp(field * (-contour_step / 4))

    def fill(i, _):
        for kind in range(2):
            u_ref[kind, own_at + i] = gain(fields[kind, i])
        for at, mine, other in (
            (swap_at, f_swap, g_swap),
            (here_at, piece, piece_core),
            (there_at, piece_chip, piece_both),
        ):
            u_ref[core, at + i] = gain(mine[i])
            u_ref[1 - core, at + i] = gain(other[i])

    lax.fori_loop(0, block, fill, None)

    def shift(i, _):
        for kind in range(2):
            u_left_ref[kind, i], u_right_ref[kind, i] = shifts(u_ref[kind, i], 1)

    lax.fori_loop(0, 4 * block, shift, None, unroll=2)


def forward_kernel(
    labels, window, swap, straight, u_ref, u_left_ref, u_right_ref,
    one_ref, low_ref, high_ref, keep_ref, send_ref,
    q_ref, product_ref, *scratch,
):
    arms, block = swap.shape[0], swap.shape[1]
    side = lax.rem(lax.axis_index("space"), 2)
    core = lax.rem(lax.axis_index("arm"), 2)
    own_at, swap_at, straight_at, across_at = places(block)

    def fill(i, _):
        for j in range(arms):
            q_ref[j, own_at + i] = window[j, i]
            q_ref[j, across_at + i] = window[arms + j, i]
            q_ref[j, swap_at + i] = swap[j, i]
            q_ref[j, straight_at + i] = straight[j, i]

    lax.fori_loop(0, block, fill, None)
    kinds = [labels[side * arms + j] for j in range(arms)]

    def factor(j, i):
        return u_ref[kinds[j], i]

    def factor_shifts(j, i):
        return u_left_ref[kinds[j], i], u_right_ref[kinds[j], i]

    def values(j, i):
        return q_ref[j, i]

    def store(j, i, value):
        q_ref[j, i] = value

    def middle(j, i, value):
        middle_ref[j, i] = value

    *scratch, middle_ref = scratch
    two_steps(block, arms, factor, factor_shifts, values, middle, store, scratch)
    for j in range(arms):
        one_ref[j] = middle_ref[j, block : 3 * block]

    def finish(i, _):
        low, high = q_ref[0, block + i], q_ref[0, 2 * block + i]
        low_ref[0, i], high_ref[0, i] = low, high
        for j in range(1, arms):
            low_next, high_next = q_ref[j, block + i], q_ref[j, 2 * block + i]
            low_ref[j, i], high_ref[j, i] = low_next, high_next
            low, high = low * low_next, high * high_next
        product_ref[0, i], product_ref[1, i] = low, high
        keep_ref[i] = product_ref[core, i]
        send_ref[i] = product_ref[1 - core, i]

    lax.fori_loop(0, block, finish, None)


def backward_kernel(
    labels, u_ref, u_left_ref, u_right_ref, one_ref, two_left, two_low, two_high, two_right,
    j_mine, j_other, j_halo, j_halo_other,
    keep_ref, send_ref,
    junction_ref, q_ref, density_ref, middle_ref, *scratch,
):
    arms, block = two_low.shape[0], two_low.shape[1]
    side = lax.rem(lax.axis_index("space"), 2)
    core = lax.rem(lax.axis_index("arm"), 2)
    kinds = [labels[side * arms + j] for j in range(arms)]

    def fill(i, _):
        junction_ref[block + core * block + i] = j_mine[i]
        junction_ref[2 * block - core * block + i] = j_other[i]
        junction_ref[3 * block * (1 - core) + i] = j_halo[i]
        junction_ref[3 * block * core + i] = j_halo_other[i]
        for place, two in enumerate((two_left, two_low, two_high, two_right)):
            whole = junction_ref[place * block + i]
            for j in range(arms):
                q_ref[j, place * block + i] = whole / two[j, i]

    lax.fori_loop(0, block, fill, None)

    def factor(j, i):
        return u_ref[kinds[j], i]

    def factor_shifts(j, i):
        return u_left_ref[kinds[j], i], u_right_ref[kinds[j], i]

    def values(j, i):
        return q_ref[j, i]

    def store(j, i, value):
        q_ref[j, i] = value

    def middle(j, i, value):
        middle_ref[j, i] = value

    two_steps(block, arms, factor, factor_shifts, values, middle, store, scratch)

    is_a = [(kind == 0).astype(jnp.float32) for kind in kinds]

    def segment(i, _):
        quarter = 0.25 * junction_ref[block + i]
        total_a = total_b = None
        for j in range(arms):
            value = 0.5 * one_ref[j, i] * middle_ref[j, block + i] + 0.25 * q_ref[j, block + i] + quarter
            part_a, part_b = is_a[j] * value, (1.0 - is_a[j]) * value
            total_a = part_a if j == 0 else total_a + part_a
            total_b = part_b if j == 0 else total_b + part_b
        density_ref[0, i], density_ref[1, i] = total_a, total_b

    lax.fori_loop(0, 2 * block, segment, None)
    chips, owned = keep_ref.shape[0], keep_ref.shape[4]

    def spread(i, _):
        for chip in range(chips):
            mine = pl.ds(pl.multiple_of((2 * chip + core) * owned, 8), owned)
            other = pl.ds(pl.multiple_of((2 * chip + 1 - core) * owned, 8), owned)
            for part in range(2):
                for kind in range(2):
                    keep_ref[chip, part, kind, i] = density_ref[kind, part * block + i, mine]
                    send_ref[chip, part, kind, i] = density_ref[kind, part * block + i, other]

    lax.fori_loop(0, block, spread, None)


def product_kernel(one, other, *out_refs):
    planes = one.shape[0] // len(out_refs)
    for k, out_ref in enumerate(out_refs):
        part = slice(k * planes, (k + 1) * planes)
        out_ref[...] = one[part] * other[part]


def join_kernel(upper, upper_other, lower, lower_other, out_ref):
    planes = upper.shape[0]
    out_ref[:planes] = upper[...] * upper_other[...]
    out_ref[planes:] = lower[...] * lower_other[...]


def total_kernel(*refs):
    *blocks, total_ref = refs
    total = jnp.zeros_like(total_ref)
    for block in blocks:
        for i in range(block.shape[0]):
            total = total + jnp.sum(block[i].reshape(-1, *total_ref.shape), axis=0)
    total_ref[...] = total


def meet_kernel(keep, received, own_ref, *out_refs):
    chips = keep.shape[0]
    side = lax.rem(lax.axis_index("space"), 2)
    chip = lax.div(lax.axis_index("arm"), 2)
    own_ref[...] = keep[chip, side] + received[chip, side]
    for out_ref, (step, flip) in zip(out_refs, other_chips(chips)):
        to_chip = lax.rem(chip + step, chips)
        to_side = 1 - side if flip else side
        out_ref[...] = keep[to_chip, to_side] + received[to_chip, to_side]


def final_kernel(cell_count, arm_count, fields, total, own, *refs):
    *others, density_ref, new_ref = refs
    owned = own.shape[2]
    scale = cell_count / (arm_count * jnp.sum(total[...]))
    rows = pl.ds(pl.multiple_of(lax.axis_index("arm") * owned, 8), owned)
    density = own[...]
    for other in others:
        density = density + other[...]
    density = density * scale
    density_ref[...] = density
    field_a, field_b = fields[0, :, rows], fields[1, :, rows]
    pressure = 0.5 * (field_a + field_b - chi_value)
    new_ref[0] = field_a + mixing * (chi_value * density[1] + pressure - field_a)
    new_ref[1] = field_b + mixing * (chi_value * density[0] + pressure - field_b)


def other_chips(chips):
    return [(step, flip) for step in range(chips) for flip in (False, True) if step or flip]


def vmem(shape):
    return pltpu.VMEM(shape, jnp.float32)


def f32(shape):
    return jax.ShapeDtypeStruct(shape, jnp.float32)


def call(kernel, out_shape, scratch, smem, *args, cost=1_000_000):
    specs = [pl.BlockSpec(memory_space=pltpu.SMEM if k < smem else pltpu.VMEM) for k in range(len(args))]
    return pl.pallas_call(
        kernel,
        out_shape=out_shape,
        in_specs=specs,
        out_specs=jax.tree.map(lambda _: pl.BlockSpec(memory_space=pltpu.VMEM), out_shape),
        scratch_shapes=scratch,
        compiler_params=pltpu.CompilerParams(vmem_limit_bytes=40 * 1024 * 1024),
        cost_estimate=pl.CostEstimate(flops=cost, bytes_accessed=cost, transcendentals=0),
    )(*args)


def local(fields, starts, labels):
    arm_size, space_size = lax.axis_size("arm"), lax.axis_size("space")
    chips, pairs = arm_size // 2, space_size // 2
    held, block, rows, columns = starts.shape
    arms = held // 2
    owned = rows // arm_size
    if chips != 2 or held % 2 or space_size % 2 or block % 2:
        raise ValueError("unsupported mesh")
    side = lax.rem(lax.axis_index("space"), 2)
    core = lax.rem(lax.axis_index("arm"), 2)

    def send(value, target):
        perm = []
        for a in range(arm_size):
            for s in range(space_size):
                chip_to, core_to, pair_to, side_to = target(a // 2, a % 2, s // 2, s % 2)
                to = (2 * (chip_to % chips) + core_to) * space_size + 2 * (pair_to % pairs) + side_to
                perm.append((a * space_size + s, to))
        return lax.ppermute(value, AXES, perm)

    def to_core(value):
        return send(value, lambda x, c, p, h: (x, 1 - c, p, h))

    def to_side(value):
        return send(value, lambda x, c, p, h: (x, c, p, 1 - h))

    def to_chip(value):
        return send(value, lambda x, c, p, h: (x + 1, c, p, h))

    def to_straight(value):
        return send(value, lambda x, c, p, h: (x, c, p + 2 * h - 1, h))

    def to_across(value):
        return send(value, lambda x, c, p, h: (x, c, p + 2 * h - 1, 1 - h))

    field_own = call(pick_kernel, f32((block, rows, columns)), [], 0, fields)
    other_set, own_set = call(pack_kernel, (f32((arms, block, rows, columns)),) * 2, [], 0, starts)
    field_got = send(field_own, lambda x, c, p, h: (x, c, p + 2 * h - 1, 1 - h if x else h))
    across = to_across(other_set)
    swap = to_side(other_set)
    straight = to_straight(own_set)
    field_both = send(field_got, lambda x, c, p, h: (1 - x, 1 - c, p, h))
    pieces = [field_got, to_core(field_got), to_core(field_both), field_both]
    field_swap = to_side(field_own)
    swap_more = to_core(field_swap)

    wide = vmem((arms, 4 * block, rows, columns))
    whole = (arms, 2 * block, rows, columns)
    part = (arms, block, rows, columns)
    one = (block, rows, columns)
    window = call(window_kernel, f32((2 * arms, block, rows, columns)), [], 1, labels, starts, across)
    gains = f32((2, 4 * block, rows, columns))
    factors = call(gain_kernel, (gains,) * 3, [], 0, fields, field_swap, swap_more, *pieces)
    step_one, low, high, keep, give = call(
        forward_kernel,
        (f32(whole), f32(part), f32(part), f32(one), f32(one)),
        [wide, vmem((2,) + one)] + [wide] * 9,
        1,
        labels, window, swap, straight, *factors,
        cost=8_000_000,
    )
    right = send(low, lambda x, c, p, h: (x, c, p - 1, h))
    left = send(high, lambda x, c, p, h: (x, c, p + 1, h))
    half = f32((block // 2, rows, columns))
    upper, lower = call(product_kernel, (half, half), [], 0, keep, to_core(give))
    upper = call(product_kernel, (half,), [], 0, upper, to_side(upper))[0]
    lower = call(product_kernel, (half,), [], 0, lower, to_chip(lower))[0]
    junction = call(join_kernel, f32(one), [], 0, upper, to_chip(upper), lower, to_side(lower))
    halo = send(junction, lambda x, c, p, h: (x, c, p + 2 * c - 1, h))
    held_junction, left, right = lax.optimization_barrier((junction, left, right))
    junction_other = to_core(held_junction)
    halo_other = to_core(halo)

    total = call(total_kernel, f32((8, columns)), [], 0, junction, junction_other, halo, halo_other, cost=1)
    if pairs & (pairs - 1) == 0:
        step = 2
        while step < pairs:
            total = total + send(total, lambda x, c, p, h, step=step: (x, c, p + step, h))
            step *= 2
    else:
        total = lax.psum(total, "space") / 4.0
    parts = (chips, 2, 2, block, owned, columns)
    keep, give = call(
        backward_kernel,
        (f32(parts), f32(parts)),
        [vmem((4 * block, rows, columns)), wide, vmem((2,) + whole[1:])] + [wide] * 9,
        1,
        labels, *factors, step_one, left, low, high, right, junction, junction_other, halo, halo_other,
        cost=8_000_000,
    )
    to_places = other_chips(chips)
    own, *gives = call(
        meet_kernel, (f32(parts[2:]),) * (1 + len(to_places)), [], 0, keep, to_core(give)
    )
    received = [
        send(value, lambda x, c, p, h, step=step, flip=flip: (x + step, c, p, 1 - h if flip else h))
        for value, (step, flip) in zip(gives, to_places)
    ]
    cell_count = block * space_size * rows * columns
    return call(
        functools.partial(final_kernel, cell_count, held * arm_size),
        (f32(parts[2:]), f32(parts[2:])),
        [],
        0,
        fields, total, own, *received,
    )


def solution(mesh):
    in_specs = (P(None, "space", None, None), P("arm", "space", None, None), P("arm"))
    out_specs = (P(None, "space", "arm", None), P(None, "space", "arm", None))
    return jax.shard_map(local, mesh=mesh, in_specs=in_specs, out_specs=out_specs, check_vma=False)
```
